256 devices in a mesh: ctx: 16 (over x, y), ksplit: 16 (over z, core).
Axes of the slice: x: 4, y: 4, z: 8, core: 2. Of those that a mesh axis runs over, the one named last changes fastest.
Arguments:
- queries: bfloat16 [8192, 32, 128], P('ctx'), may hold values from -5 to 5
- stretch_kv: bfloat16 [8192, 8, 256], P('ctx'), may hold values from -5 to 5
- prefix_kv: bfloat16 [1024, 64, 8, 256], P(('ctx', 'ksplit')), may hold values from -5 to 5
- vertical: int32 [8, 64], replicated, may hold values from 0 to 1023, as said below
- slash_offsets: int32 [32, 32], replicated, may hold values from 0 to 39, as said below
- block_home: int32 [1024], replicated, may hold values from 0 to 1023, as said below
Outputs:
- attention: bfloat16 [8192, 4096], P('ctx', 'ksplit')
The draws below stay inside these ranges and needn't reach their ends.
Inputs may be any that keep to these rules, and one draw needn't show every extreme that they name: `vertical`: each row names 64 different prefix blocks; entry j names a block whose slot, divided by 4, is a device number d of ctx+ksplit with d mod 16 = j mod 16. `slash_offsets`: each row holds 32 different offsets, 0 among them. `block_home`: A permutation.
All inputs are finite; a program needn't handle non-finite values.
Results may differ from the reference program's by a relative error of at most 0.0055.
Values may be sent and summed in bfloat16 or wider, within the bound.
A program may use at most 192 MiB of HBM per device.

```python
import jax
import jax.numpy as jnp
from jax import lax

QUERY_HEADS = 32
KV_HEADS = 8
HEAD_SIZE = 128
BLOCK = 64
VERTICAL = 64
SLASH = 32
SPAN = 40
PREFIX_DEV = 4
STRETCH_BLOCKS = 128
STRETCH = 8192
PREFIX_BLOCKS = 1024
N_CTX = 16
N_KSPLIT = 16


def home_slots(key):
    return jax.random.permutation(key, PREFIX_BLOCKS).astype(jnp.int32)


def draw_queries(key, part):
    key = jax.random.fold_in(key, 11)
    drawn = jax.random.normal(key, (STRETCH, QUERY_HEADS, HEAD_SIZE))
    return jnp.clip(drawn, -5.0, 5.0).astype(jnp.bfloat16)


def draw_stretch_kv(key, part):
    key = jax.random.fold_in(key, 12)
    values = jax.random.normal(jax.random.fold_in(key, 1), (STRETCH, KV_HEADS, HEAD_SIZE))
    keys_part = jax.random.normal(key, (STRETCH, KV_HEADS, HEAD_SIZE))
    joined = jnp.concatenate([jnp.clip(keys_part, -5.0, 5.0), jnp.clip(values, -5.0, 5.0)], -1)
    return joined.astype(jnp.bfloat16)


def draw_block_home(key, part):
    return home_slots(key)


def draw_vertical(key, part):
    slots_of = home_slots(key)
    key = jax.random.fold_in(key, 2)
    per_column = N_CTX * PREFIX_DEV
    shares = VERTICAL // N_KSPLIT
    subkeys = jax.random.split(key, KV_HEADS * N_KSPLIT)
    picked = jax.vmap(lambda subkey: jax.random.permutation(subkey, per_column)[:shares])(subkeys)
    picked = picked.reshape(KV_HEADS, N_KSPLIT, shares).astype(jnp.int32)
    column = jnp.arange(N_KSPLIT, dtype=jnp.int32)[None, :, None]
    slot_ids = (picked // PREFIX_DEV * N_KSPLIT + column) * PREFIX_DEV + picked % PREFIX_DEV
    block_of = jnp.zeros((PREFIX_BLOCKS,), jnp.int32).at[slots_of].set(jnp.arange(PREFIX_BLOCKS, dtype=jnp.int32))
    blocks = block_of[slot_ids]
    return jnp.transpose(blocks, (0, 2, 1)).reshape(KV_HEADS, VERTICAL).astype(jnp.int32)


def draw_slash_offsets(key, part):
    key = jax.random.fold_in(key, 3)
    subkeys = jax.random.split(key, QUERY_HEADS)
    others = jax.vmap(lambda subkey: jax.random.permutation(subkey, SPAN - 1)[:SLASH - 1] + 1)(subkeys)
    return jnp.concatenate([jnp.zeros((QUERY_HEADS, 1), jnp.int32), others.astype(jnp.int32)], 1)


def block_levels(key, shape, shards, low, largest):
    loudness = 1.0
    for axis_at, shards_of in shards:
        steps = jax.random.uniform(jax.random.fold_in(jax.random.fold_in(key, 6), axis_at), (shards_of,), jnp.float32, low / len(shards), largest / len(shards))
        loudness = loudness * jnp.repeat(jnp.exp(steps), shape[axis_at] // shards_of).reshape((-1,) + (1,) * (len(shape) - 1 - axis_at))
    return loudness


def normal_values(key, dims, deviation, reach, shards=(), kind=jnp.bfloat16):
    values = jax.random.normal(key, dims, jnp.float32) * deviation
    if len(shards) > 0:
        values = block_levels(key, dims, shards, -0.22, 0.18) * values
    return jnp.clip(values, min=-reach, max=reach).astype(kind)


def setup_inputs(seed: int = 0) -> dict:
    key_of = jax.random.split(jax.random.key(seed), 7)
    queries = draw_queries(jax.random.fold_in(key_of[6], 71), 0)
    stretch_kv = draw_stretch_kv(jax.random.fold_in(key_of[6], 71), 0)
    prefix_kv = normal_values(key_of[2], (PREFIX_BLOCKS, BLOCK, KV_HEADS, 2 * HEAD_SIZE), 1.0, 5.0, ((0, 256),))
    vertical = draw_vertical(jax.random.fold_in(key_of[6], 71), 0)
    slash_offsets = draw_slash_offsets(jax.random.fold_in(key_of[6], 71), 0)
    block_home = draw_block_home(jax.random.fold_in(key_of[6], 71), 0)
    return {"queries": queries, "stretch_kv": stretch_kv, "prefix_kv": prefix_kv, "vertical": vertical, "slash_offsets": slash_offsets, "block_home": block_home}


def rounded_length(values):
    return lax.optimization_barrier(values.astype(jnp.bfloat16)).astype(jnp.float32)


def reference(queries, stretch_kv, prefix_kv, vertical, slash_offsets, block_home):
    group_size = QUERY_HEADS // KV_HEADS
    own_heads = QUERY_HEADS // N_KSPLIT
    shares = VERTICAL // N_KSPLIT
    score_scale = 1.0 / (HEAD_SIZE ** 0.5)
    entries = vertical.reshape(KV_HEADS, shares, N_KSPLIT)
    slot_ids = block_home[entries]
    head_index = jnp.arange(KV_HEADS).astype(jnp.int32)[:, None, None]
    picked = prefix_kv[slot_ids, :, head_index, :]
    vertical_kv = picked.transpose(2, 0, 1, 3, 4).reshape(N_KSPLIT, KV_HEADS, shares * BLOCK, 2 * HEAD_SIZE).astype(jnp.float32)
    stretch_blocks = stretch_kv.reshape(STRETCH_BLOCKS, BLOCK, KV_HEADS, 2 * HEAD_SIZE)
    head_group = (jnp.arange(QUERY_HEADS) // group_size).astype(jnp.int32)
    owner_of = (jnp.arange(QUERY_HEADS) // own_heads).astype(jnp.int32)
    owns_slash = jnp.arange(N_KSPLIT)[:, None] == owner_of[None, :]
    position = jnp.arange(BLOCK)
    causal = position[None, :] <= position[:, None]

    def one_block(block_number):
        query_rows = lax.dynamic_slice_in_dim(queries, block_number * BLOCK, BLOCK, 0).astype(jnp.float32)
        grouped_heads = query_rows.reshape(BLOCK, KV_HEADS, group_size, HEAD_SIZE)
        vertical_scores = jnp.einsum("tghd,sgkd->sghtk", grouped_heads, vertical_kv[..., :HEAD_SIZE]) * score_scale
        vertical_scores = vertical_scores.reshape(N_KSPLIT, QUERY_HEADS, BLOCK, -1)
        block_of_keys = block_number - slash_offsets
        reachable = block_of_keys >= 0
        clipped = jnp.maximum(block_of_keys, 0).astype(jnp.int32)
        slash_key_value = stretch_blocks[clipped, :, head_group[:, None], :].astype(jnp.float32)
        slash_scores = jnp.einsum("thd,hnsd->htns", query_rows, slash_key_value[..., :HEAD_SIZE]) * score_scale
        allowed = reachable[:, None, :, None] & ((slash_offsets != 0)[:, None, :, None] | causal[None, :, None, :])
        slash_scores = jnp.where(allowed, slash_scores, -jnp.inf).reshape(QUERY_HEADS, BLOCK, -1)
        vertical_top = jnp.max(vertical_scores, 3)
        slash_top = jnp.max(slash_scores, 2)
        joint_top = jnp.where(owns_slash[..., None], jnp.maximum(vertical_top, slash_top[None]), vertical_top)
        own_top = jnp.maximum(vertical_top[owner_of, jnp.arange(QUERY_HEADS)], slash_top)
        vertical_weights = jnp.exp(vertical_scores - joint_top[..., None])
        slash_weight_matrix = jnp.exp(slash_scores - own_top[..., None])
        vertical_probs = rounded_length(vertical_weights).reshape(N_KSPLIT, KV_HEADS, group_size, BLOCK, -1)
        vertical_acc = jnp.einsum("sghtk,sgkd->sghtd", vertical_probs, vertical_kv[..., HEAD_SIZE:])
        vertical_acc = vertical_acc.reshape(N_KSPLIT, QUERY_HEADS, BLOCK, HEAD_SIZE)
        slash_accumulator = jnp.einsum("avu,auz->avz", rounded_length(slash_weight_matrix), slash_key_value[..., HEAD_SIZE:].reshape(QUERY_HEADS, -1, HEAD_SIZE))
        totals = jnp.sum(vertical_weights, 3) + jnp.where(owns_slash[..., None], jnp.sum(slash_weight_matrix, 2)[None], 0.0)
        accumulated = vertical_acc + jnp.where(owns_slash[..., None, None], slash_accumulator[None], 0.0)
        partial_lse = joint_top + jnp.log(totals)
        partial_value = rounded_length(accumulated / totals[..., None])
        lse_top = jnp.max(partial_lse, 0)
        lse_all = lse_top + jnp.log(jnp.sum(jnp.exp(partial_lse - lse_top), 0))
        weights = jnp.exp(partial_lse - lse_all)
        combined = jnp.sum(weights[..., None] * partial_value, 0)
        return combined.transpose(1, 0, 2).reshape(BLOCK, QUERY_HEADS * HEAD_SIZE).astype(jnp.bfloat16)

    blocks = lax.map(one_block, jnp.arange(STRETCH_BLOCKS).astype(jnp.int32))
    return blocks.reshape(STRETCH, QUERY_HEADS * HEAD_SIZE)
```

```python
import functools
import math

import jax
import jax.numpy as jnp
from jax import lax
from jax.experimental import pallas as pl
from jax.experimental.pallas import tpu as pltpu
from jax.sharding import PartitionSpec as P

MESH = pl.DeviceIdType.MESH
BLOCK = 64
NX = 4
NY = 4
NZ = 8
HOPS = 5
MASKED = -1e30
SCALE = math.log2(math.e) / math.sqrt(128.0)
BAND = 42 * BLOCK
SLASH_CHUNK = 896
F32 = jnp.float32
BF16 = jnp.bfloat16


def iota(shape, dim):
    return lax.broadcasted_iota(jnp.int32, shape, dim)


def kernel(
    q_hbm, s_hbm, p_hbm, vertical, offsets, home, out,
    xq, xs, xp, contrib, r1, p1, r2, fin, zr, vert, win, qb, band, acc, top,
    load_sem, r1_send, r1_recv, r2_send, r2_recv, z_send, z_recv,
    g1_send, g1_recv, g2_send, g2_recv, v_send, v_recv, w_send, w_recv, f_send, f_recv,
):
    c = lax.axis_index("ctx")
    s = lax.axis_index("ksplit")
    x, y = c // NY, c % NY
    z, core = s // 2, s % 2

    load_p = pltpu.make_async_copy(p_hbm, xp, load_sem.at[0])
    load_s = pltpu.make_async_copy(s_hbm, xs, load_sem.at[1])
    slab = pl.multiple_of((s // 8) * 16, 16)
    load_q = pltpu.make_async_copy(q_hbm.at[:, pl.ds(slab, 16), :], xq, load_sem.at[2])
    load_p.start()
    load_s.start()
    load_q.start()

    barrier = pltpu.get_barrier_semaphore()
    for k in range(1, NX * NY):
        pl.semaphore_signal(barrier, inc=1, device_id=((c + k) % (NX * NY), s), device_id_type=MESH)
    for k in range(1, NZ):
        pl.semaphore_signal(barrier, inc=1, device_id=(c, ((z + k) % NZ) * 2 + core), device_id_type=MESH)
    pl.semaphore_signal(barrier, inc=1, device_id=(c, z * 2 + 1 - core), device_id_type=MESH)

    me = c * (2 * NZ) + s
    row16 = iota((16, 256), 0) % 8
    codes = []
    for v in range(4):
        code = jnp.full((16, 256), -1, jnp.int32)
        for g in range(8):
            slot = home[vertical[g, v * 2 * NZ + s]]
            here = jnp.where(slot // 4 == me, slot % 4, -1)
            code = jnp.where(row16 == g, here, code)
        codes.append(code)

    load_p.wait()
    for v in range(4):
        total = None
        for r in range(4):
            keep = jnp.where(codes[v] == r, 1.0, 0.0).astype(BF16)
            term = xp[pl.ds(r * 512, 512), :].reshape(32, 16, 256) * keep[None]
            total = term if total is None else total + term
        contrib[v] = total.reshape(512, 256)

    pl.semaphore_wait(barrier, NX * NY - 1 + NZ - 1 + 1)

    def along_x(k):
        return (((x + k) % NX) * NY + y, s)

    def along_y(k):
        return (x * NY + (y + k) % NY, s)

    sibling = (c, z * 2 + 1 - core)

    def remote(src, dst, send, recv, to):
        return pltpu.make_async_remote_copy(
            src_ref=src, dst_ref=dst, send_sem=send, recv_sem=recv, device_id=to, device_id_type=MESH
        )

    def first_round(half, k):
        to = along_x(k) if half == 0 else along_y(k)
        part = (x + k) % NX if half == 0 else (y + k) % NY
        src = contrib.at[pl.ds(2 * half, 2), pl.ds(pl.multiple_of(part * 128, 128), 128), :]
        return remote(src, r1.at[half, k - 1], r1_send.at[half, k - 1], r1_recv.at[half, k - 1], to)

    def second_round(half, k):
        to = along_y(k) if half == 0 else along_x(k)
        part = (y + k) % NY if half == 0 else (x + k) % NX
        src = p1.at[half, :, pl.ds(pl.multiple_of(part * 32, 32), 32), :]
        return remote(src, r2.at[half, k - 1], r2_send.at[half, k - 1], r2_recv.at[half, k - 1], to)

    order = (2, 1, 3)
    sends = []
    for k in order:
        for half in range(2):
            copy = first_round(half, k)
            copy.start()
            sends.append(copy)

    load_s.wait()
    pick_kv = jnp.where(iota((64, 512), 1) == iota((64, 512), 0) * 8 + z, 1.0, 0.0).astype(BF16)
    for b in range(8):
        picked = jnp.dot(pick_kv, xs[pl.ds(b * 512, 512), :], preferred_element_type=F32)
        win[pl.ds(HOPS * 512 + b * 64, 64), :] = picked.astype(BF16)

    def window_copy(d):
        half = pl.multiple_of(core * 256, 256)
        return remote(
            win.at[pl.ds(HOPS * 512 + half, 256), :],
            win.at[pl.ds((HOPS - d) * 512 + half, 256), :],
            w_send.at[d - 1], w_recv.at[d - 1], ((c + d) % (NX * NY), s),
        )

    def window_swap(d):
        part = win.at[pl.ds((HOPS - d) * 512 + pl.multiple_of(core * 256, 256), 256), :]
        return remote(part, part, f_send.at[d - 1], f_recv.at[d - 1], sibling)

    load_q.wait()
    i, j = iota((128, 1024), 0), iota((128, 1024), 1)
    pick_q = jnp.where(j == (i % 64) * 16 + 2 * (s % 8) + i // 64, 1.0, 0.0).astype(BF16)
    for b in range(8):
        slab_rows = xq[pl.ds(b * 64, 64)].reshape(1024, 128)
        qb[b] = jnp.dot(pick_q, slab_rows, preferred_element_type=F32).astype(BF16)

    rows = iota((8, BAND), 0)
    offset = 40 + (rows // 2) % 2 - iota((8, BAND), 1) // 64
    member = jnp.full((8, BAND), MASKED, F32)
    for n in range(32):
        first, second = offsets[2 * s, n], offsets[2 * s + 1, n]
        member = jnp.where(offset == jnp.where(rows % 2 == 0, first, second), 0.0, member)
    band[...] = member

    for half in range(2):
        part = x if half == 0 else y
        total = contrib[pl.ds(2 * half, 2), pl.ds(pl.multiple_of(part * 128, 128), 128), :]
        for k in order:
            first_round(half, k).wait_recv()
            total = total + r1[half, k - 1]
        p1[half] = total
        for k in order:
            copy = second_round(half, k)
            copy.start()
            sends.append(copy)
    for d in (2, 5, 3, 1, 4):
        copy = window_copy(d)
        copy.start()
        sends.append(copy)

    ends = []
    for half in range(2):
        part = y if half == 0 else x
        total = p1[half, :, pl.ds(pl.multiple_of(part * 32, 32), 32), :]
        for k in order:
            second_round(half, k).wait_recv()
            total = total + r2[half, k - 1]
        ends.append(total.reshape(64, 256))
    held = jnp.concatenate(ends, 0)
    i, j = iota((128, 128), 0), iota((128, 128), 1)
    by_head = jnp.where(i == (j % 8) * 16 + (j // 32) * 4 + (j % 32) // 8, 1.0, 0.0).astype(BF16)
    fin[...] = jnp.dot(by_head, held, preferred_element_type=F32).astype(BF16)

    def z_copy(k):
        there = (z + k) % NZ
        return remote(
            fin.at[pl.ds(pl.multiple_of(there * 16, 16), 16), :],
            zr.at[pl.ds(pl.multiple_of(z * 16, 16), 16), :],
            z_send.at[k - 1], z_recv.at[k - 1], (c, there * 2 + core),
        )

    def z_arrival(k):
        there = (z + NZ - k) % NZ
        place = zr.at[pl.ds(pl.multiple_of(there * 16, 16), 16), :]
        return remote(place, place, z_send.at[k - 1], z_recv.at[k - 1], (c, there * 2 + core))

    for k in (4, 3, 5, 2, 6, 1, 7):
        copy = z_copy(k)
        copy.start()
        sends.append(copy)
    mine = pl.ds(pl.multiple_of(z * 16, 16), 16)
    zr[mine, :] = fin[mine, :]
    for k in range(1, NZ):
        z_arrival(k).wait_recv()

    def place(owner, half, outer, inner, count=64):
        start = ((owner * 2 + half) * 16 + outer * 4 + inner) * 64
        return vert.at[pl.ds(pl.multiple_of(start, 64), count), :]

    def spread_one(half, k):
        outer, inner = (x, y) if half == 0 else (y, x)
        part = place(core, half, outer, inner)
        to = along_y(k) if half == 0 else along_x(k)
        return remote(part, part, g1_send.at[half, k - 1], g1_recv.at[half, k - 1], to)

    def spread_one_arrival(half, k):
        outer, inner = (x, (y + 4 - k) % 4) if half == 0 else (y, (x + 4 - k) % 4)
        part = place(core, half, outer, inner)
        to = along_y(k) if half == 0 else along_x(k)
        return remote(part, part, g1_send.at[half, k - 1], g1_recv.at[half, k - 1], to)

    def spread_two(half, k):
        outer = x if half == 0 else y
        part = place(core, half, outer, 0, 256)
        to = along_x(k) if half == 0 else along_y(k)
        return remote(part, part, g2_send.at[half, k - 1], g2_recv.at[half, k - 1], to)

    def spread_two_arrival(half, k):
        outer = ((x if half == 0 else y) + 4 - k) % 4
        part = place(core, half, outer, 0, 256)
        to = along_x(k) if half == 0 else along_y(k)
        return remote(part, part, g2_send.at[half, k - 1], g2_recv.at[half, k - 1], to)

    def swap(half, k):
        outer = ((x if half == 0 else y) + 4 - k) % 4
        part = place(core, half, outer, 0, 256)
        return remote(part, part, v_send.at[half, k], v_recv.at[half, k], sibling)

    def swap_arrival(half, k):
        outer = ((x if half == 0 else y) + 4 - k) % 4
        part = place(1 - core, half, outer, 0, 256)
        return remote(part, part, v_send.at[half, k], v_recv.at[half, k], sibling)

    for half in range(2):
        outer, inner = (x, y) if half == 0 else (y, x)
        start = pl.multiple_of(((core * 2 + half) * 16 + outer * 4 + inner) * 64, 64)
        vert[pl.ds(start, 64), :] = zr[pl.ds(half * 64, 64), :]
        for k in order:
            copy = spread_one(half, k)
            copy.start()
            sends.append(copy)
    for half in range(2):
        for k in order:
            spread_one_arrival(half, k).wait_recv()
        for k in order:
            copy = spread_two(half, k)
            copy.start()
            sends.append(copy)
        copy = swap(half, 0)
        copy.start()
        sends.append(copy)

    for d in range(1, HOPS + 1):
        window_copy(d).wait_recv()
        copy = window_swap(d)
        copy.start()
        sends.append(copy)
    for d in range(1, HOPS + 1):
        part = win.at[pl.ds((HOPS - d) * 512 + pl.multiple_of((1 - core) * 256, 256), 256), :]
        remote(part, part, f_send.at[d - 1], f_recv.at[d - 1], sibling).wait_recv()

    acc[...] = jnp.zeros(acc.shape, F32)
    top[...] = jnp.full(top.shape, MASKED, F32)
    ones = {}

    def attend(pair, keys, bias, last):
        rows = pl.ds(pl.multiple_of(pair * 256, 256), 256)
        q = qb[pl.ds(pair * 2, 2)].reshape(256, 128)
        n = keys.shape[0]
        scores = lax.dot_general(q, keys[:, :128], (((1,), (1,)), ((), ())), preferred_element_type=F32)
        if bias is not None:
            wide = [jnp.broadcast_to(bias[r : r + 1], (64, n)) for r in range(4)]
            scores = scores + jnp.concatenate(wide, 0)
            if last:
                i, j = iota((256, 128), 0), iota((256, 128), 1)
                later = (j // 64 == i // 128) & (j % 64 > i % 64)
                tail = scores[:, n - 128 :] + jnp.where(later, MASKED, 0.0)
                scores = jnp.concatenate([scores[:, : n - 128], tail], 1)
        old = top[rows, :]
        new = jnp.maximum(old, jnp.max(scores, 1, keepdims=True))
        top[rows, :] = new
        probs = jnp.exp2((scores - new[:, :1]) * SCALE).astype(BF16)
        fade = jnp.exp2((old - new) * SCALE)
        values = jnp.concatenate([keys[:, 128:], jnp.ones((n, 128), BF16)], 1)
        add = jnp.dot(probs, values, preferred_element_type=F32)
        acc[rows, :] = acc[rows, :] * jnp.concatenate([fade, fade], 1) + add

    def slash_pair(pair, _):
        for chunk in range(BAND // SLASH_CHUNK):
            start = pl.multiple_of(pair * 128 + chunk * SLASH_CHUNK, 128)
            lanes = pl.ds(chunk * SLASH_CHUNK, SLASH_CHUNK)
            block = c * 8 - 40 + 2 * pair + (iota((8, SLASH_CHUNK), 1) + chunk * SLASH_CHUNK) // 64
            bias = band[:, lanes] + jnp.where(block >= 0, 0.0, MASKED)
            attend(pair, win[pl.ds(start, SLASH_CHUNK), :], bias, chunk == BAND // SLASH_CHUNK - 1)
        return 0

    lax.fori_loop(0, 4, slash_pair, 0)

    for k in order:
        for half in range(2):
            spread_two_arrival(half, k).wait_recv()
            copy = swap(half, k)
            copy.start()
            sends.append(copy)
    for k in (0,) + order:
        for half in range(2):
            swap_arrival(half, k).wait_recv()

    def vertical_pair(pair, _):
        for chunk in range(4):
            attend(pair, vert[pl.ds(chunk * 1024, 1024), :], None, False)
        return 0

    lax.fori_loop(0, 4, vertical_pair, 0)

    for b in range(8):
        for h in range(2):
            rows = pl.ds(b * 128 + h * 64, 64)
            out[pl.ds(b * 64, 64), pl.ds(h * 128, 128)] = (acc[rows, :128] / acc[rows, 128:]).astype(BF16)

    for copy in sends:
        copy.wait_send()


def on_device(queries, stretch_kv, prefix_kv, vertical, slash_offsets, block_home):
    anywhere = pl.BlockSpec(memory_space=pl.ANY)
    scalars = pl.BlockSpec(memory_space=pltpu.SMEM)
    dma = pltpu.SemaphoreType.DMA
    return pl.pallas_call(
        kernel,
        out_shape=jax.ShapeDtypeStruct((512, 256), BF16),
        in_specs=[anywhere] * 3 + [scalars] * 3,
        out_specs=pl.BlockSpec(memory_space=pltpu.VMEM),
        scratch_shapes=[
            pltpu.VMEM((512, 16, 128), BF16),
            pltpu.VMEM((4096, 256), BF16),
            pltpu.VMEM((2048, 256), BF16),
            pltpu.VMEM((4, 512, 256), BF16),
            pltpu.VMEM((2, 3, 2, 128, 256), BF16),
            pltpu.VMEM((2, 2, 128, 256), BF16),
            pltpu.VMEM((2, 3, 2, 32, 256), BF16),
            pltpu.VMEM((128, 256), BF16),
            pltpu.VMEM((128, 256), BF16),
            pltpu.VMEM((4096, 256), BF16),
            pltpu.VMEM(((HOPS + 1) * 512, 256), BF16),
            pltpu.VMEM((8, 128, 128), BF16),
            pltpu.VMEM((8, BAND), F32),
            pltpu.VMEM((1024, 256), F32),
            pltpu.VMEM((1024, 128), F32),
            dma((3,)),
            dma((2, 3)), dma((2, 3)),
            dma((2, 3)), dma((2, 3)),
            dma((NZ - 1,)), dma((NZ - 1,)),
            dma((2, 3)), dma((2, 3)),
            dma((2, 3)), dma((2, 3)),
            dma((2, 4)), dma((2, 4)),
            dma((HOPS,)), dma((HOPS,)),
            dma((HOPS,)), dma((HOPS,)),
        ],
        compiler_params=pltpu.CompilerParams(
            collective_id=0, has_side_effects=True, vmem_limit_bytes=48 * 1024 * 1024
        ),
        cost_estimate=pl.CostEstimate(flops=7_000_000_000, bytes_accessed=6_000_000, transcendentals=7_000_000),
    )(
        queries,
        stretch_kv.reshape(-1, 256),
        prefix_kv.reshape(-1, 256),
        vertical,
        slash_offsets,
        block_home,
    )


def solution(mesh):
    return jax.shard_map(
        on_device,
        mesh=mesh,
        in_specs=(
            P("ctx", None, None),
            P("ctx", None, None),
            P(("ctx", "ksplit"), None, None, None),
            P(),
            P(),
            P(),
        ),
        out_specs=P("ctx", "ksplit"),
        check_vma=False,
    )
```

```python
import functools
import math

import jax
import jax.numpy as jnp
from jax import lax
from jax.experimental import pallas as pl
from jax.experimental.pallas import tpu as pltpu
from jax.sharding import PartitionSpec as P

MESH = pl.DeviceIdType.MESH
BLOCK = 64
NX = 4
NY = 4
NZ = 8
HOPS = 5
MASKED = -1e30
SCALE = math.log2(math.e) / math.sqrt(128.0)
BAND = 42 * BLOCK
F32 = jnp.float32
BF16 = jnp.bfloat16


def iota(shape, dim):
    return lax.broadcasted_iota(jnp.int32, shape, dim)


def kernel(
    q_hbm, s_hbm, p_hbm, vertical, offsets, home, out,
    xq, xs, xp, contrib, r1, p1, r2, fin, zr, vert, win, qb, band, acc, top,
    load_sem, r1_send, r1_recv, r2_send, r2_recv, z_send, z_recv,
    g1_send, g1_recv, g2_send, g2_recv, v_send, v_recv, w_send, w_recv, f_send, f_recv,
):
    c = lax.axis_index("ctx")
    s = lax.axis_index("ksplit")
    x, y = c // NY, c % NY
    z, core = s // 2, s % 2

    barrier = pltpu.get_barrier_semaphore()
    for k in range(1, 4):
        pl.semaphore_signal(barrier, inc=1, device_id=(((x + k) % NX) * NY + y, s), device_id_type=MESH)
        pl.semaphore_signal(barrier, inc=1, device_id=(x * NY + (y + k) % NY, s), device_id_type=MESH)
    for k in range(1, NZ):
        pl.semaphore_signal(barrier, inc=1, device_id=(c, ((z + k) % NZ) * 2 + core), device_id_type=MESH)
    pl.semaphore_signal(barrier, inc=1, device_id=(c, z * 2 + 1 - core), device_id_type=MESH)

    load_p = pltpu.make_async_copy(p_hbm, xp, load_sem.at[0])
    load_s = pltpu.make_async_copy(s_hbm, xs, load_sem.at[1])
    slab = pl.multiple_of((s // 8) * 16, 16)
    load_q = pltpu.make_async_copy(q_hbm.at[:, pl.ds(slab, 16), :], xq, load_sem.at[2])
    load_p.start()
    load_s.start()
    load_q.start()

    me = c * (2 * NZ) + s
    row16 = iota((16, 256), 0) % 8
    codes = []
    for v in range(4):
        code = jnp.full((16, 256), -1, jnp.int32)
        for g in range(8):
            slot = home[vertical[g, v * 2 * NZ + s]]
            here = jnp.where(slot // 4 == me, slot % 4, -1)
            code = jnp.where(row16 == g, here, code)
        codes.append(code)

    load_p.wait()
    for v in range(4):
        total = None
        for r in range(4):
            keep = jnp.where(codes[v] == r, 1.0, 0.0).astype(BF16)
            term = xp[pl.ds(r * 512, 512), :].reshape(32, 16, 256) * keep[None]
            total = term if total is None else total + term
        contrib[v] = total.reshape(512, 256)

    pl.semaphore_wait(barrier, 3 + 3 + NZ - 1 + 1)

    def along_x(k):
        return (((x + k) % NX) * NY + y, s)

    def along_y(k):
        return (x * NY + (y + k) % NY, s)

    sibling = (c, z * 2 + 1 - core)

    def remote(src, dst, send, recv, to):
        return pltpu.make_async_remote_copy(
            src_ref=src, dst_ref=dst, send_sem=send, recv_sem=recv, device_id=to, device_id_type=MESH
        )

    def first_round(half, k):
        to = along_x(k) if half == 0 else along_y(k)
        part = (x + k) % NX if half == 0 else (y + k) % NY
        src = contrib.at[pl.ds(2 * half, 2), pl.ds(pl.multiple_of(part * 128, 128), 128), :]
        return remote(src, r1.at[half, k - 1], r1_send.at[half, k - 1], r1_recv.at[half, k - 1], to)

    def second_round(half, k):
        to = along_y(k) if half == 0 else along_x(k)
        part = (y + k) % NY if half == 0 else (x + k) % NX
        src = p1.at[half, :, pl.ds(pl.multiple_of(part * 32, 32), 32), :]
        return remote(src, r2.at[half, k - 1], r2_send.at[half, k - 1], r2_recv.at[half, k - 1], to)

    order = (2, 1, 3)
    sends = []
    for k in order:
        for half in range(2):
            copy = first_round(half, k)
            copy.start()
            sends.append(copy)

    load_s.wait()
    pick_kv = jnp.where(iota((64, 512), 1) == iota((64, 512), 0) * 8 + z, 1.0, 0.0).astype(BF16)
    for b in range(8):
        picked = jnp.dot(pick_kv, xs[pl.ds(b * 512, 512), :], preferred_element_type=F32)
        win[pl.ds(HOPS * 512 + b * 64, 64), :] = picked.astype(BF16)

    def window_part(d, which):
        return win.at[pl.ds(pl.multiple_of((HOPS - d) * 512 + which * 256, 256), 256), :]

    def window_copy(d, held):
        to = along_x(1) if d >= 4 else along_y(d)
        return remote(window_part(held, core), window_part(d, core), w_send.at[d - 1], w_recv.at[d - 1], to)

    def window_arrival(d):
        return window_copy(d, d)

    def window_swap(d, which):
        part = window_part(d, which)
        return remote(part, part, f_send.at[d - 1], f_recv.at[d - 1], sibling)

    load_q.wait()
    i, j = iota((128, 1024), 0), iota((128, 1024), 1)
    pick_q = jnp.where(j == (i % 64) * 16 + 2 * (s % 8) + i // 64, 1.0, 0.0).astype(BF16)
    for b in range(8):
        slab_rows = xq[pl.ds(b * 64, 64)].reshape(1024, 128)
        qb[b] = jnp.dot(pick_q, slab_rows, preferred_element_type=F32).astype(BF16)

    rows = iota((8, BAND), 0)
    offset = 40 + (rows // 2) % 2 - iota((8, BAND), 1) // 64
    member = jnp.full((8, BAND), MASKED, F32)
    for n in range(32):
        first, second = offsets[2 * s, n], offsets[2 * s + 1, n]
        member = jnp.where(offset == jnp.where(rows % 2 == 0, first, second), 0.0, member)
    band[...] = member

    for half in range(2):
        part = x if half == 0 else y
        total = contrib[pl.ds(2 * half, 2), pl.ds(pl.multiple_of(part * 128, 128), 128), :]
        for k in order:
            first_round(half, k).wait_recv()
            total = total + r1[half, k - 1]
        p1[half] = total
        for k in order:
            copy = second_round(half, k)
            copy.start()
            sends.append(copy)
    copy = window_copy(4, 0)
    copy.start()
    sends.append(copy)
    for d in (1, 2, 3):

        @pl.when(y + d < NY)
        def _(d=d):
            window_copy(d, 0).start()


    ends = []
    for half in range(2):
        part = y if half == 0 else x
        total = p1[half, :, pl.ds(pl.multiple_of(part * 32, 32), 32), :]
        for k in order:
            second_round(half, k).wait_recv()
            total = total + r2[half, k - 1]
        ends.append(total.reshape(64, 256))
    held = jnp.concatenate(ends, 0)
    i, j = iota((128, 128), 0), iota((128, 128), 1)
    by_head = jnp.where(i == (j % 8) * 16 + (j // 32) * 4 + (j % 32) // 8, 1.0, 0.0).astype(BF16)
    fin[...] = jnp.dot(by_head, held, preferred_element_type=F32).astype(BF16)

    def z_copy(k):
        there = (z + k) % NZ
        return remote(
            fin.at[pl.ds(pl.multiple_of(there * 16, 16), 16), :],
            zr.at[pl.ds(pl.multiple_of(z * 16, 16), 16), :],
            z_send.at[k - 1], z_recv.at[k - 1], (c, there * 2 + core),
        )

    def z_arrival(k):
        there = (z + NZ - k) % NZ
        place = zr.at[pl.ds(pl.multiple_of(there * 16, 16), 16), :]
        return remote(place, place, z_send.at[k - 1], z_recv.at[k - 1], (c, there * 2 + core))

    for k in (4, 3, 5, 2, 6, 1, 7):
        copy = z_copy(k)
        copy.start()
        sends.append(copy)
    window_arrival(4).wait_recv()
    for d in (1, 2, 3):

        @pl.when(y + d >= NY)
        def _(d=d):
            window_copy(d, 4).start()

        sends.append(window_copy(d, 0))
    copy = window_swap(4, core)
    copy.start()
    sends.append(copy)
    mine = pl.ds(pl.multiple_of(z * 16, 16), 16)
    zr[mine, :] = fin[mine, :]
    for k in range(1, NZ):
        z_arrival(k).wait_recv()

    def place(k, owner, half, start, count):
        return vert.at[pl.ds(pl.multiple_of(((k * 2 + owner) * 2 + half) * 256 + start, 64), count), :]

    def spread_one(half, k):
        to = along_y(k) if half == 0 else along_x(k)
        dst = place(0, core, half, k * 64, 64)
        return remote(place(0, core, half, 0, 64), dst, g1_send.at[half, k - 1], g1_recv.at[half, k - 1], to)

    def spread_two(half, k):
        to = along_x(k) if half == 0 else along_y(k)
        dst = place(k, core, half, 0, 256)
        return remote(place(0, core, half, 0, 256), dst, g2_send.at[half, k - 1], g2_recv.at[half, k - 1], to)

    def swap(half, k, owner):
        part = place(k, owner, half, 0, 256)
        return remote(part, part, v_send.at[half, k], v_recv.at[half, k], sibling)

    def start_swap(k):
        for half in range(2):
            copy = swap(half, k, core)
            copy.start()
            sends.append(copy)

    def end_swap(k):
        for half in range(2):
            swap(half, k, 1 - core).wait_recv()

    def arrive(k):
        for half in range(2):
            spread_two(half, k).wait_recv()
        start_swap(k)

    for half in range(2):
        start = pl.multiple_of((core * 2 + half) * 256, 256)
        vert[pl.ds(start, 64), :] = zr[pl.ds(half * 64, 64), :]
        for k in order:
            copy = spread_one(half, k)
            copy.start()
            sends.append(copy)

    def attend(b, keys, bias=None, diagonal=False, first=False):
        rows = pl.ds(b * 128, 128)
        n = keys.shape[0]
        scores = lax.dot_general(qb[b], keys[:, :128], (((1,), (1,)), ((), ())), preferred_element_type=F32)
        if bias is not None:
            wide = [jnp.broadcast_to(bias[r : r + 1], (64, n)) for r in (2 * (b % 2), 2 * (b % 2) + 1)]
            scores = scores + jnp.concatenate(wide, 0)
        if diagonal:
            i, j = iota((128, 128), 0), iota((128, 128), 1)
            later = (j // 64 == b % 2) & (j % 64 > i % 64)
            tail = scores[:, n - 128 :] + jnp.where(later, MASKED, 0.0)
            scores = jnp.concatenate([scores[:, : n - 128], tail], 1)
        new = jnp.max(scores, 1, keepdims=True)
        if not first:
            old = top[rows, :]
            new = jnp.maximum(old, new)
        probs = jnp.exp2((scores - new[:, :1]) * SCALE).astype(BF16)
        values = jnp.concatenate([keys[:, 128:], jnp.ones((n, 128), BF16)], 1)
        add = jnp.dot(probs, values, preferred_element_type=F32)
        if first:
            top[rows, :] = jnp.broadcast_to(new, (128, 128))
            acc[rows, :] = add
        else:
            fade = jnp.exp2((old - new) * SCALE)
            top[rows, :] = new
            acc[rows, :] = acc[rows, :] * jnp.concatenate([fade, fade], 1) + add

    def band_part(start, count, d):
        return band[:, pl.ds(start, count)] + jnp.where(c >= d, 0.0, MASKED)

    def slash_near():
        for b in range(8):
            p = b // 2
            keys = jnp.concatenate([win[pl.ds(512, 512), :], win[pl.ds(2560, 128 * p + 128), :]], 0)
            bias = [band_part(512 - 128 * p, 512, 4), band_part(2560 - 128 * p, 128 * p + 128, 0)]
            attend(b, keys, jnp.concatenate(bias, 1), diagonal=True, first=True)

    def slash_middle():
        for b in range(8):
            p = b // 2
            bias = [band_part(1024 - 128 * p, 512, 3), band_part(1536 - 128 * p, 512, 2)]
            attend(b, win[pl.ds(1024, 1024), :], jnp.concatenate(bias, 1))

    def slash_far():
        for b in range(8):
            p = b // 2
            keys = jnp.concatenate([win[pl.ds(128 * p, 512 - 128 * p), :], win[pl.ds(2048, 512), :]], 0)
            bias = [band_part(0, 512 - 128 * p, 5), band_part(2048 - 128 * p, 512, 1)]
            attend(b, keys, jnp.concatenate(bias, 1))

    def vertical_step(k):
        for b in range(8):
            attend(b, vert[pl.ds(k * 1024, 1024), :])

    window_swap(4, 1 - core).wait_recv()
    slash_near()

    for half in range(2):
        for k in order:
            spread_one(half, k).wait_recv()
        for k in (1, 3, 2):
            copy = spread_two(half, k)
            copy.start()
            sends.append(copy)
    start_swap(0)
    for d in (1, 2, 3):
        window_arrival(d).wait_recv()
        if d == 1:
            copy = window_copy(5, 1)
            copy.start()
            sends.append(copy)
        copy = window_swap(d, core)
        copy.start()
        sends.append(copy)

    for d in (2, 3):
        window_swap(d, 1 - core).wait_recv()
    slash_middle()
    end_swap(0)
    vertical_step(0)
    arrive(1)
    arrive(3)
    window_arrival(5).wait_recv()
    copy = window_swap(5, core)
    copy.start()
    sends.append(copy)
    end_swap(1)
    vertical_step(1)
    for d in (1, 5):
        window_swap(d, 1 - core).wait_recv()
    slash_far()
    arrive(2)
    end_swap(3)
    vertical_step(3)
    end_swap(2)
    vertical_step(2)

    for b in range(8):
        for h in range(2):
            rows = pl.ds(b * 128 + h * 64, 64)
            out[pl.ds(b * 64, 64), pl.ds(h * 128, 128)] = (acc[rows, :128] / acc[rows, 128:]).astype(BF16)

    for copy in sends:
        copy.wait_send()


def on_device(queries, stretch_kv, prefix_kv, vertical, slash_offsets, block_home):
    anywhere = pl.BlockSpec(memory_space=pl.ANY)
    scalars = pl.BlockSpec(memory_space=pltpu.SMEM)
    dma = pltpu.SemaphoreType.DMA
    return pl.pallas_call(
        kernel,
        out_shape=jax.ShapeDtypeStruct((512, 256), BF16),
        in_specs=[anywhere] * 3 + [scalars] * 3,
        out_specs=pl.BlockSpec(memory_space=pltpu.VMEM),
        scratch_shapes=[
            pltpu.VMEM((512, 16, 128), BF16),
            pltpu.VMEM((4096, 256), BF16),
            pltpu.VMEM((2048, 256), BF16),
            pltpu.VMEM((4, 512, 256), BF16),
            pltpu.VMEM((2, 3, 2, 128, 256), BF16),
            pltpu.VMEM((2, 2, 128, 256), BF16),
            pltpu.VMEM((2, 3, 2, 32, 256), BF16),
            pltpu.VMEM((128, 256), BF16),
            pltpu.VMEM((128, 256), BF16),
            pltpu.VMEM((4096, 256), BF16),
            pltpu.VMEM(((HOPS + 1) * 512, 256), BF16),
            pltpu.VMEM((8, 128, 128), BF16),
            pltpu.VMEM((8, BAND), F32),
            pltpu.VMEM((1024, 256), F32),
            pltpu.VMEM((1024, 128), F32),
            dma((3,)),
            dma((2, 3)), dma((2, 3)),
            dma((2, 3)), dma((2, 3)),
            dma((NZ - 1,)), dma((NZ - 1,)),
            dma((2, 3)), dma((2, 3)),
            dma((2, 3)), dma((2, 3)),
            dma((2, 4)), dma((2, 4)),
            dma((HOPS,)), dma((HOPS,)),
            dma((HOPS,)), dma((HOPS,)),
        ],
        compiler_params=pltpu.CompilerParams(
            collective_id=0, has_side_effects=True, vmem_limit_bytes=62 * 1024 * 1024
        ),
        cost_estimate=pl.CostEstimate(flops=7_000_000_000, bytes_accessed=6_000_000, transcendentals=7_000_000),
    )(
        queries,
        stretch_kv.reshape(-1, 256),
        prefix_kv.reshape(-1, 256),
        vertical,
        slash_offsets,
        block_home,
    )


def solution(mesh):
    return jax.shard_map(
        on_device,
        mesh=mesh,
        in_specs=(
            P("ctx", None, None),
            P("ctx", None, None),
            P(("ctx", "ksplit"), None, None, None),
            P(),
            P(),
            P(),
        ),
        out_specs=P("ctx", "ksplit"),
        check_vma=False,
    )
```

```python
import functools
import math

import jax
import jax.numpy as jnp
from jax import lax
from jax.experimental import pallas as pl
from jax.experimental.pallas import tpu as pltpu
from jax.sharding import PartitionSpec as P

MESH = pl.DeviceIdType.MESH
BLOCK = 64
NX = 4
NY = 4
NZ = 8
HOPS = 5
MASKED = -1e30
SCALE = math.log2(math.e) / math.sqrt(128.0)
BAND = 42 * BLOCK
F32 = jnp.float32
BF16 = jnp.bfloat16


def iota(shape, dim):
    return lax.broadcasted_iota(jnp.int32, shape, dim)


def kernel(
    q_hbm, s_hbm, p_hbm, vertical_hbm, offsets_hbm, home_hbm, out,
    vertical, offsets, home, xq, xs, xp, contrib, r1, p1, r2, fin, zr, vert, win, qb, band, acc, top,
    load_sem, r1_send, r1_recv, r2_send, r2_recv, z_send, z_recv,
    g1_send, g1_recv, g2_send, g2_recv, v_send, v_recv, w_send, w_recv, f_send, f_recv,
):
    c = lax.axis_index("ctx")
    s = lax.axis_index("ksplit")
    x, y = c // NY, c % NY
    z, core = s // 2, s % 2

    barrier = pltpu.get_barrier_semaphore()
    for k in range(1, 4):
        pl.semaphore_signal(barrier, inc=1, device_id=(((x + k) % NX) * NY + y, s), device_id_type=MESH)
        pl.semaphore_signal(barrier, inc=1, device_id=(x * NY + (y + k) % NY, s), device_id_type=MESH)
    for k in range(1, NZ):
        pl.semaphore_signal(barrier, inc=1, device_id=(c, ((z + k) % NZ) * 2 + core), device_id_type=MESH)
    pl.semaphore_signal(barrier, inc=1, device_id=(c, z * 2 + 1 - core), device_id_type=MESH)

    load_p = pltpu.make_async_copy(p_hbm, xp, load_sem.at[0])
    load_s = pltpu.make_async_copy(s_hbm, xs, load_sem.at[1])
    slab = pl.multiple_of((s // 8) * 16, 16)
    load_q = pltpu.make_async_copy(q_hbm.at[:, pl.ds(slab, 16), :], xq, load_sem.at[2])
    load_home = pltpu.make_async_copy(home_hbm, home, load_sem.at[3])
    load_vertical = pltpu.make_async_copy(vertical_hbm, vertical, load_sem.at[4])
    load_offsets = pltpu.make_async_copy(offsets_hbm, offsets, load_sem.at[5])
    load_home.start()
    load_vertical.start()
    load_offsets.start()
    load_p.start()
    load_s.start()
    load_q.start()

    load_home.wait()
    load_vertical.wait()
    load_offsets.wait()
    me = c * (2 * NZ) + s
    row16 = iota((16, 256), 0) % 8
    codes = []
    for v in range(4):
        code = jnp.full((16, 256), -1, jnp.int32)
        for g in range(8):
            slot = home[vertical[g, v * 2 * NZ + s]]
            here = jnp.where(slot // 4 == me, slot % 4, -1)
            code = jnp.where(row16 == g, here, code)
        codes.append(code)

    load_p.wait()
    for v in range(4):
        total = None
        for r in range(4):
            keep = jnp.where(codes[v] == r, 1.0, 0.0).astype(BF16)
            term = xp[pl.ds(r * 512, 512), :].reshape(32, 16, 256) * keep[None]
            total = term if total is None else total + term
        contrib[v] = total.reshape(512, 256)

    pl.semaphore_wait(barrier, 3 + 3 + NZ - 1 + 1)

    def along_x(k):
        return (((x + k) % NX) * NY + y, s)

    def along_y(k):
        return (x * NY + (y + k) % NY, s)

    sibling = (c, z * 2 + 1 - core)

    def remote(src, dst, send, recv, to):
        return pltpu.make_async_remote_copy(
            src_ref=src, dst_ref=dst, send_sem=send, recv_sem=recv, device_id=to, device_id_type=MESH
        )

    def first_round(half, k):
        to = along_x(k) if half == 0 else along_y(k)
        part = (x + k) % NX if half == 0 else (y + k) % NY
        src = contrib.at[pl.ds(2 * half, 2), pl.ds(pl.multiple_of(part * 128, 128), 128), :]
        return remote(src, r1.at[half, k - 1], r1_send.at[half, k - 1], r1_recv.at[half, k - 1], to)

    def second_round(half, k):
        to = along_y(k) if half == 0 else along_x(k)
        part = (y + k) % NY if half == 0 else (x + k) % NX
        src = p1.at[half, :, pl.ds(pl.multiple_of(part * 32, 32), 32), :]
        return remote(src, r2.at[half, k - 1], r2_send.at[half, k - 1], r2_recv.at[half, k - 1], to)

    order = (2, 1, 3)
    sends = []
    for k in order:
        for half in range(2):
            first_round(half, k).start()

    load_s.wait()
    pick_kv = jnp.where(iota((64, 512), 1) == iota((64, 512), 0) * 8 + z, 1.0, 0.0).astype(BF16)
    for b in range(8):
        picked = jnp.dot(pick_kv, xs[pl.ds(b * 512, 512), :], preferred_element_type=F32)
        win[pl.ds(HOPS * 512 + b * 64, 64), :] = picked.astype(BF16)

    def window_part(d, which):
        return win.at[pl.ds(pl.multiple_of((HOPS - d) * 512 + which * 256, 256), 256), :]

    def window_copy(d, held):
        to = along_x(1) if d >= 4 else along_y(d)
        return remote(window_part(held, core), window_part(d, core), w_send.at[d - 1], w_recv.at[d - 1], to)

    def window_arrival(d):
        return window_copy(d, d)

    def window_swap(d, which):
        part = window_part(d, which)
        return remote(part, part, f_send.at[d - 1], f_recv.at[d - 1], sibling)

    load_q.wait()
    i, j = iota((128, 1024), 0), iota((128, 1024), 1)
    pick_q = jnp.where(j == (i % 64) * 16 + 2 * (s % 8) + i // 64, 1.0, 0.0).astype(BF16)
    for b in range(8):
        slab_rows = xq[pl.ds(b * 64, 64)].reshape(1024, 128)
        qb[b] = jnp.dot(pick_q, slab_rows, preferred_element_type=F32).astype(BF16)

    rows = iota((8, BAND), 0)
    offset = 40 + (rows // 2) % 2 - iota((8, BAND), 1) // 64
    member = jnp.full((8, BAND), MASKED, F32)
    for n in range(32):
        first, second = offsets[2 * s, n], offsets[2 * s + 1, n]
        member = jnp.where(offset == jnp.where(rows % 2 == 0, first, second), 0.0, member)
    band[...] = member

    for half in range(2):
        for k in order:
            first_round(half, k).wait_send()
    for half in range(2):
        part = x if half == 0 else y
        total = contrib[pl.ds(2 * half, 2), pl.ds(pl.multiple_of(part * 128, 128), 128), :]
        for k in order:
            first_round(half, k).wait_recv()
            total = total + r1[half, k - 1]
        p1[half] = total
        for k in order:
            copy = second_round(half, k)
            copy.start()
            sends.append(copy)
    copy = window_copy(4, 0)
    copy.start()
    sends.append(copy)

    ends = []
    for half in range(2):
        part = y if half == 0 else x
        total = p1[half, :, pl.ds(pl.multiple_of(part * 32, 32), 32), :]
        for k in order:
            second_round(half, k).wait_recv()
            total = total + r2[half, k - 1]
        ends.append(total.reshape(64, 256))
    held = jnp.concatenate(ends, 0)
    i, j = iota((128, 128), 0), iota((128, 128), 1)
    by_head = jnp.where(i == (j % 8) * 16 + (j // 32) * 4 + (j % 32) // 8, 1.0, 0.0).astype(BF16)
    fin[...] = jnp.dot(by_head, held, preferred_element_type=F32).astype(BF16)

    def z_copy(k):
        there = (z + k) % NZ
        return remote(
            fin.at[pl.ds(pl.multiple_of(there * 16, 16), 16), :],
            zr.at[pl.ds(pl.multiple_of(z * 16, 16), 16), :],
            z_send.at[k - 1], z_recv.at[k - 1], (c, there * 2 + core),
        )

    def z_arrival(k):
        there = (z + NZ - k) % NZ
        place = zr.at[pl.ds(pl.multiple_of(there * 16, 16), 16), :]
        return remote(place, place, z_send.at[k - 1], z_recv.at[k - 1], (c, there * 2 + core))

    for k in (4, 3, 5, 2, 6, 1, 7):
        copy = z_copy(k)
        copy.start()
        sends.append(copy)
    mine = pl.ds(pl.multiple_of(z * 16, 16), 16)
    zr[mine, :] = fin[mine, :]
    for k in range(1, NZ):
        z_arrival(k).wait_recv()

    def place(k, owner, half, start, count):
        return vert.at[pl.ds(pl.multiple_of(((k * 2 + owner) * 2 + half) * 256 + start, 64), count), :]

    def spread_one(half, k):
        to = along_y(k) if half == 0 else along_x(k)
        dst = place(0, core, half, k * 64, 64)
        return remote(place(0, core, half, 0, 64), dst, g1_send.at[half, k - 1], g1_recv.at[half, k - 1], to)

    def spread_two(half, k):
        to = along_x(k) if half == 0 else along_y(k)
        dst = place(k, core, half, 0, 256)
        return remote(place(0, core, half, 0, 256), dst, g2_send.at[half, k - 1], g2_recv.at[half, k - 1], to)

    def swap(half, k, owner):
        part = place(k, owner, half, 0, 256)
        return remote(part, part, v_send.at[half, k], v_recv.at[half, k], sibling)

    def start_swap(k):
        for half in range(2):
            copy = swap(half, k, core)
            copy.start()
            sends.append(copy)

    def end_swap(k):
        for half in range(2):
            swap(half, k, 1 - core).wait_recv()

    def arrive(k):
        for half in range(2):
            spread_two(half, k).wait_recv()
        start_swap(k)

    for half in range(2):
        start = pl.multiple_of((core * 2 + half) * 256, 256)
        vert[pl.ds(start, 64), :] = zr[pl.ds(half * 64, 64), :]
        for k in order:
            copy = spread_one(half, k)
            copy.start()
            sends.append(copy)

    window_arrival(4).wait_recv()
    for d in (1, 2, 3):
        copy = window_copy(d, jnp.where(y + d < NY, 0, 4))
        copy.start()
        sends.append(copy)
    copy = window_swap(4, core)
    copy.start()
    sends.append(copy)
    def attend(b, keys, bias=None, diagonal=False, first=False):
        rows = pl.ds(b * 128, 128)
        n = keys.shape[0]
        scores = lax.dot_general(qb[b], keys[:, :128], (((1,), (1,)), ((), ())), preferred_element_type=F32)
        if bias is not None:
            wide = [jnp.broadcast_to(bias[r : r + 1], (64, n)) for r in (2 * (b % 2), 2 * (b % 2) + 1)]
            scores = scores + jnp.concatenate(wide, 0)
        if diagonal:
            i, j = iota((128, 128), 0), iota((128, 128), 1)
            later = (j // 64 == b % 2) & (j % 64 > i % 64)
            tail = scores[:, n - 128 :] + jnp.where(later, MASKED, 0.0)
            scores = jnp.concatenate([scores[:, : n - 128], tail], 1)
        new = jnp.max(scores, 1, keepdims=True)
        if not first:
            old = top[rows, :]
            new = jnp.maximum(old, new)
        probs = jnp.exp2((scores - new[:, :1]) * SCALE).astype(BF16)
        values = jnp.concatenate([keys[:, 128:], jnp.ones((n, 128), BF16)], 1)
        add = jnp.dot(probs, values, preferred_element_type=F32)
        if first:
            top[rows, :] = jnp.broadcast_to(new, (128, 128))
            acc[rows, :] = add
        else:
            fade = jnp.exp2((old - new) * SCALE)
            top[rows, :] = new
            acc[rows, :] = acc[rows, :] * jnp.concatenate([fade, fade], 1) + add

    def band_part(start, count, d):
        return band[:, pl.ds(start, count)] + jnp.where(c >= d, 0.0, MASKED)

    def slash_near():
        for b in range(8):
            p = b // 2
            keys = jnp.concatenate([win[pl.ds(512, 512), :], win[pl.ds(2560, 128 * p + 128), :]], 0)
            bias = [band_part(512 - 128 * p, 512, 4), band_part(2560 - 128 * p, 128 * p + 128, 0)]
            attend(b, keys, jnp.concatenate(bias, 1), diagonal=True, first=True)

    def slash_middle():
        for b in range(8):
            p = b // 2
            bias = [band_part((1 + i) * 512 + 512 - 128 * p, 512, 3 - i) for i in range(3)]
            attend(b, win[pl.ds(1024, 1536), :], jnp.concatenate(bias, 1))

    def slash_far():
        for b in range(8):
            p = b // 2
            attend(b, win[pl.ds(128 * p, 512 - 128 * p), :], band_part(0, 512 - 128 * p, 5))

    def vertical_step(k):
        for b in range(8):
            attend(b, vert[pl.ds(k * 1024, 1024), :])

    window_swap(4, 1 - core).wait_recv()
    slash_near()

    for half in range(2):
        for k in order:
            spread_one(half, k).wait_recv()
        for k in (1, 3, 2):
            copy = spread_two(half, k)
            copy.start()
            sends.append(copy)
    start_swap(0)
    window_arrival(1).wait_recv()
    copy = window_copy(5, 1)
    copy.start()
    sends.append(copy)
    end_swap(0)
    vertical_step(0)
    for d in (1, 3, 2):
        if d > 1:
            window_arrival(d).wait_recv()
        copy = window_swap(d, core)
        copy.start()
        sends.append(copy)
    arrive(1)
    arrive(3)
    for d in (1, 2, 3):
        window_swap(d, 1 - core).wait_recv()
    slash_middle()
    end_swap(1)
    vertical_step(1)
    window_arrival(5).wait_recv()
    copy = window_swap(5, core)
    copy.start()
    sends.append(copy)
    arrive(2)
    end_swap(3)
    vertical_step(3)
    window_swap(5, 1 - core).wait_recv()
    slash_far()
    end_swap(2)
    vertical_step(2)

    for b in range(8):
        for h in range(2):
            rows = pl.ds(b * 128 + h * 64, 64)
            out[pl.ds(b * 64, 64), pl.ds(h * 128, 128)] = (acc[rows, :128] / acc[rows, 128:]).astype(BF16)

    for copy in sends:
        copy.wait_send()


def on_device(queries, stretch_kv, prefix_kv, vertical, slash_offsets, block_home):
    anywhere = pl.BlockSpec(memory_space=pl.ANY)
    dma = pltpu.SemaphoreType.DMA
    return pl.pallas_call(
        kernel,
        out_shape=jax.ShapeDtypeStruct((512, 256), BF16),
        in_specs=[anywhere] * 6,
        out_specs=pl.BlockSpec(memory_space=pltpu.VMEM),
        scratch_shapes=[
            pltpu.SMEM((8, 64), jnp.int32),
            pltpu.SMEM((32, 32), jnp.int32),
            pltpu.SMEM((1024,), jnp.int32),
            pltpu.VMEM((512, 16, 128), BF16),
            pltpu.VMEM((4096, 256), BF16),
            pltpu.VMEM((2048, 256), BF16),
            pltpu.VMEM((4, 512, 256), BF16),
            pltpu.VMEM((2, 3, 2, 128, 256), BF16),
            pltpu.VMEM((2, 2, 128, 256), BF16),
            pltpu.VMEM((2, 3, 2, 32, 256), BF16),
            pltpu.VMEM((128, 256), BF16),
            pltpu.VMEM((128, 256), BF16),
            pltpu.VMEM((4096, 256), BF16),
            pltpu.VMEM(((HOPS + 1) * 512, 256), BF16),
            pltpu.VMEM((8, 128, 128), BF16),
            pltpu.VMEM((8, BAND), F32),
            pltpu.VMEM((1024, 256), F32),
            pltpu.VMEM((1024, 128), F32),
            dma((6,)),
            dma((2, 3)), dma((2, 3)),
            dma((2, 3)), dma((2, 3)),
            dma((NZ - 1,)), dma((NZ - 1,)),
            dma((2, 3)), dma((2, 3)),
            dma((2, 3)), dma((2, 3)),
            dma((2, 4)), dma((2, 4)),
            dma((HOPS,)), dma((HOPS,)),
            dma((HOPS,)), dma((HOPS,)),
        ],
        compiler_params=pltpu.CompilerParams(
            collective_id=0, has_side_effects=True, vmem_limit_bytes=62 * 1024 * 1024
        ),
        cost_estimate=pl.CostEstimate(flops=7_000_000_000, bytes_accessed=6_000_000, transcendentals=7_000_000),
    )(
        queries,
        stretch_kv.reshape(-1, 256),
        prefix_kv.reshape(-1, 256),
        vertical,
        slash_offsets,
        block_home,
    )


def solution(mesh):
    return jax.shard_map(
        on_device,
        mesh=mesh,
        in_specs=(
            P("ctx", None, None),
            P("ctx", None, None),
            P(("ctx", "ksplit"), None, None, None),
            P(),
            P(),
            P(),
        ),
        out_specs=P("ctx", "ksplit"),
        check_vma=False,
    )
```

```python
import functools
import math

import jax
import jax.numpy as jnp
from jax import lax
from jax.experimental import pallas as pl
from jax.experimental.pallas import tpu as pltpu
from jax.sharding import PartitionSpec as P

MESH = pl.DeviceIdType.MESH
BLOCK = 64
NX = 4
NY = 4
NZ = 8
HOPS = 5
MASKED = -1e30
SCALE = math.log2(math.e) / math.sqrt(128.0)
BAND = 42 * BLOCK
F32 = jnp.float32
BF16 = jnp.bfloat16


def iota(shape, dim):
    return lax.broadcasted_iota(jnp.int32, shape, dim)


def kernel(
    q_hbm, s_hbm, p_hbm, vertical_hbm, offsets_hbm, home_hbm, out,
    vertical, offsets, home, xq, xs, xp, contrib, r1, p1, r2, fin, zr, vert, win, qb, band, acc, top,
    load_sem, r1_send, r1_recv, r2_send, r2_recv, z_send, z_recv,
    g1_send, g1_recv, g2_send, g2_recv, v_send, v_recv, w_send, w_recv, f_send, f_recv,
):
    c = lax.axis_index("ctx")
    s = lax.axis_index("ksplit")
    x, y = c // NY, c % NY
    z, core = s // 2, s % 2

    barrier = pltpu.get_barrier_semaphore()
    for k in range(1, 4):
        pl.semaphore_signal(barrier, inc=1, device_id=(((x + k) % NX) * NY + y, s), device_id_type=MESH)
        pl.semaphore_signal(barrier, inc=1, device_id=(x * NY + (y + k) % NY, s), device_id_type=MESH)
    for k in range(1, NZ):
        pl.semaphore_signal(barrier, inc=1, device_id=(c, ((z + k) % NZ) * 2 + core), device_id_type=MESH)
    pl.semaphore_signal(barrier, inc=1, device_id=(c, z * 2 + 1 - core), device_id_type=MESH)

    load_p = pltpu.make_async_copy(p_hbm, xp, load_sem.at[0])
    load_s = pltpu.make_async_copy(s_hbm, xs, load_sem.at[1])
    slab = pl.multiple_of((s // 8) * 16, 16)
    load_q = pltpu.make_async_copy(q_hbm.at[:, pl.ds(slab, 16), :], xq, load_sem.at[2])
    load_home = pltpu.make_async_copy(home_hbm, home, load_sem.at[3])
    load_vertical = pltpu.make_async_copy(vertical_hbm, vertical, load_sem.at[4])
    load_offsets = pltpu.make_async_copy(offsets_hbm, offsets, load_sem.at[5])
    load_home.start()
    load_vertical.start()
    load_offsets.start()
    load_p.start()
    load_s.start()
    load_q.start()

    load_home.wait()
    load_vertical.wait()
    load_offsets.wait()
    me = c * (2 * NZ) + s
    row16 = iota((16, 256), 0) % 8
    codes = []
    for v in range(4):
        code = jnp.full((16, 256), -1, jnp.int32)
        for g in range(8):
            slot = home[vertical[g, v * 2 * NZ + s]]
            here = jnp.where(slot // 4 == me, slot % 4, -1)
            code = jnp.where(row16 == g, here, code)
        codes.append(code)

    load_p.wait()
    for v in range(4):
        total = None
        for r in range(4):
            keep = jnp.where(codes[v] == r, 1.0, 0.0).astype(BF16)
            term = xp[pl.ds(r * 512, 512), :].reshape(32, 16, 256) * keep[None]
            total = term if total is None else total + term
        contrib[v] = total.reshape(512, 256)

    pl.semaphore_wait(barrier, 3 + 3 + NZ - 1 + 1)

    def along_x(k):
        return (((x + k) % NX) * NY + y, s)

    def along_y(k):
        return (x * NY + (y + k) % NY, s)

    sibling = (c, z * 2 + 1 - core)

    def remote(src, dst, send, recv, to):
        return pltpu.make_async_remote_copy(
            src_ref=src, dst_ref=dst, send_sem=send, recv_sem=recv, device_id=to, device_id_type=MESH
        )

    def first_round(half, k):
        to = along_x(k) if half == 0 else along_y(k)
        part = (x + k) % NX if half == 0 else (y + k) % NY
        src = contrib.at[pl.ds(2 * half, 2), pl.ds(pl.multiple_of(part * 128, 128), 128), :]
        return remote(src, r1.at[half, k - 1], r1_send.at[half, k - 1], r1_recv.at[half, k - 1], to)

    def second_round(half, k):
        to = along_y(k) if half == 0 else along_x(k)
        part = (y + k) % NY if half == 0 else (x + k) % NX
        src = p1.at[half, :, pl.ds(pl.multiple_of(part * 32, 32), 32), :]
        return remote(src, r2.at[half, k - 1], r2_send.at[half, k - 1], r2_recv.at[half, k - 1], to)

    order = (2, 1, 3)
    sends = []
    for k in order:
        for half in range(2):
            first_round(half, k).start()

    load_s.wait()
    pick_kv = jnp.where(iota((64, 512), 1) == iota((64, 512), 0) * 8 + z, 1.0, 0.0).astype(BF16)
    for b in range(8):
        picked = jnp.dot(pick_kv, xs[pl.ds(b * 512, 512), :], preferred_element_type=F32)
        win[pl.ds(HOPS * 512 + b * 64, 64), :] = picked.astype(BF16)

    def window_part(d, which):
        return win.at[pl.ds(pl.multiple_of((HOPS - d) * 512 + which * 256, 256), 256), :]

    def window_copy(d, held):
        to = along_x(1) if d >= 4 else along_y(d)
        return remote(window_part(held, core), window_part(d, core), w_send.at[d - 1], w_recv.at[d - 1], to)

    def window_arrival(d):
        return window_copy(d, d)

    def window_swap(d, which):
        part = window_part(d, which)
        return remote(part, part, f_send.at[d - 1], f_recv.at[d - 1], sibling)

    load_q.wait()
    i, j = iota((128, 1024), 0), iota((128, 1024), 1)
    pick_q = jnp.where(j == (i % 64) * 16 + 2 * (s % 8) + i // 64, 1.0, 0.0).astype(BF16)
    for b in range(8):
        slab_rows = xq[pl.ds(b * 64, 64)].reshape(1024, 128)
        qb[b] = jnp.dot(pick_q, slab_rows, preferred_element_type=F32).astype(BF16)

    rows = iota((8, BAND), 0)
    offset = 40 + (rows // 2) % 2 - iota((8, BAND), 1) // 64
    member = jnp.full((8, BAND), MASKED, F32)
    for n in range(32):
        first, second = offsets[2 * s, n], offsets[2 * s + 1, n]
        member = jnp.where(offset == jnp.where(rows % 2 == 0, first, second), 0.0, member)
    band[...] = member

    for half in range(2):
        for k in order:
            first_round(half, k).wait_send()
    copy = window_copy(4, 0)
    copy.start()
    sends.append(copy)
    for half in range(2):
        part = x if half == 0 else y
        total = contrib[pl.ds(2 * half, 2), pl.ds(pl.multiple_of(part * 128, 128), 128), :]
        for k in order:
            first_round(half, k).wait_recv()
            total = total + r1[half, k - 1]
        p1[half] = total
        for k in order:
            copy = second_round(half, k)
            copy.start()
            sends.append(copy)

    ends = []
    for half in range(2):
        part = y if half == 0 else x
        total = p1[half, :, pl.ds(pl.multiple_of(part * 32, 32), 32), :]
        for k in order:
            second_round(half, k).wait_recv()
            total = total + r2[half, k - 1]
        ends.append(total.reshape(64, 256))
    held = jnp.concatenate(ends, 0)
    i, j = iota((128, 128), 0), iota((128, 128), 1)
    by_head = jnp.where(i == (j % 8) * 16 + (j // 32) * 4 + (j % 32) // 8, 1.0, 0.0).astype(BF16)
    fin[...] = jnp.dot(by_head, held, preferred_element_type=F32).astype(BF16)

    def z_copy(k):
        there = (z + k) % NZ
        return remote(
            fin.at[pl.ds(pl.multiple_of(there * 16, 16), 16), :],
            zr.at[pl.ds(pl.multiple_of(z * 16, 16), 16), :],
            z_send.at[k - 1], z_recv.at[k - 1], (c, there * 2 + core),
        )

    def z_arrival(k):
        there = (z + NZ - k) % NZ
        place = zr.at[pl.ds(pl.multiple_of(there * 16, 16), 16), :]
        return remote(place, place, z_send.at[k - 1], z_recv.at[k - 1], (c, there * 2 + core))

    for k in (4, 3, 5, 2, 6, 1, 7):
        copy = z_copy(k)
        copy.start()
        sends.append(copy)
    def place(k, owner, half, start, count):
        return vert.at[pl.ds(pl.multiple_of(((k * 2 + owner) * 2 + half) * 256 + start, 64), count), :]

    def spread_one(half, k):
        to = along_y(k) if half == 0 else along_x(k)
        dst = place(0, core, half, k * 64, 64)
        return remote(place(0, core, half, 0, 64), dst, g1_send.at[half, k - 1], g1_recv.at[half, k - 1], to)

    def spread_two(half, k):
        to = along_x(k) if half == 0 else along_y(k)
        dst = place(k, core, half, 0, 256)
        return remote(place(0, core, half, 0, 256), dst, g2_send.at[half, k - 1], g2_recv.at[half, k - 1], to)

    def swap(half, k, owner):
        part = place(k, owner, half, 0, 256)
        return remote(part, part, v_send.at[half, k], v_recv.at[half, k], sibling)

    def start_swap(k):
        for half in range(2):
            copy = swap(half, k, core)
            copy.start()
            sends.append(copy)

    def end_swap(k):
        for half in range(2):
            swap(half, k, 1 - core).wait_recv()

    def arrive(k):
        for half in range(2):
            spread_two(half, k).wait_recv()
        start_swap(k)

    def attend(b, keys, bias=None, diagonal=False, first=False):
        rows = pl.ds(b * 128, 128)
        n = keys.shape[0]
        scores = lax.dot_general(qb[b], keys[:, :128], (((1,), (1,)), ((), ())), preferred_element_type=F32)
        if bias is not None:
            wide = [jnp.broadcast_to(bias[r : r + 1], (64, n)) for r in (2 * (b % 2), 2 * (b % 2) + 1)]
            scores = scores + jnp.concatenate(wide, 0)
        if diagonal:
            i, j = iota((128, 128), 0), iota((128, 128), 1)
            later = (j // 64 == b % 2) & (j % 64 > i % 64)
            tail = scores[:, n - 128 :] + jnp.where(later, MASKED, 0.0)
            scores = jnp.concatenate([scores[:, : n - 128], tail], 1)
        new = jnp.max(scores, 1, keepdims=True)
        if not first:
            old = top[rows, :]
            new = jnp.maximum(old, new)
        probs = jnp.exp2((scores - new[:, :1]) * SCALE).astype(BF16)
        values = jnp.concatenate([keys[:, 128:], jnp.ones((n, 128), BF16)], 1)
        add = jnp.dot(probs, values, preferred_element_type=F32)
        if first:
            top[rows, :] = jnp.broadcast_to(new, (128, 128))
            acc[rows, :] = add
        else:
            fade = jnp.exp2((old - new) * SCALE)
            top[rows, :] = new
            acc[rows, :] = acc[rows, :] * jnp.concatenate([fade, fade], 1) + add

    def band_part(start, count, d):
        return band[:, pl.ds(start, count)] + jnp.where(c >= d, 0.0, MASKED)

    def slash_near():
        for b in range(8):
            p = b // 2
            keys = jnp.concatenate([win[pl.ds(512, 512), :], win[pl.ds(2560, 128 * p + 128), :]], 0)
            bias = [band_part(512 - 128 * p, 512, 4), band_part(2560 - 128 * p, 128 * p + 128, 0)]
            attend(b, keys, jnp.concatenate(bias, 1), diagonal=True, first=True)

    def slash_middle():
        for b in range(8):
            p = b // 2
            bias = [band_part(1024 - 128 * p, 512, 3), band_part(1536 - 128 * p, 512, 2)]
            attend(b, win[pl.ds(1024, 1024), :], jnp.concatenate(bias, 1))

    def slash_far():
        for b in range(8):
            p = b // 2
            keys = jnp.concatenate([win[pl.ds(128 * p, 512 - 128 * p), :], win[pl.ds(2048, 512), :]], 0)
            bias = [band_part(0, 512 - 128 * p, 5), band_part(2048 - 128 * p, 512, 1)]
            attend(b, keys, jnp.concatenate(bias, 1))

    def vertical_step(k):
        for b in range(8):
            attend(b, vert[pl.ds(k * 1024, 1024), :])

    window_arrival(4).wait_recv()
    copy = window_copy(1, jnp.where(y + 1 < NY, 0, 4))
    copy.start()
    sends.append(copy)
    copy = window_copy(3, jnp.where(y + 3 < NY, 0, 4))
    copy.start()
    sends.append(copy)
    copy = window_swap(4, core)
    copy.start()
    sends.append(copy)
    mine = pl.ds(pl.multiple_of(z * 16, 16), 16)
    zr[mine, :] = fin[mine, :]
    for k in range(1, NZ):
        z_arrival(k).wait_recv()

    for half in range(2):
        start = pl.multiple_of((core * 2 + half) * 256, 256)
        vert[pl.ds(start, 64), :] = zr[pl.ds(half * 64, 64), :]
        for k in order:
            copy = spread_one(half, k)
            copy.start()
            sends.append(copy)

    copy = window_copy(2, jnp.where(y + 2 < NY, 0, 4))
    copy.start()
    sends.append(copy)
    window_arrival(1).wait_recv()
    copy = window_copy(5, 1)
    copy.start()
    sends.append(copy)
    copy = window_swap(1, core)
    copy.start()
    sends.append(copy)
    window_swap(4, 1 - core).wait_recv()
    slash_near()
    for half in range(2):
        for k in order:
            spread_one(half, k).wait_recv()
        for k in (1, 3, 2):
            copy = spread_two(half, k)
            copy.start()
            sends.append(copy)
    start_swap(0)
    window_arrival(3).wait_recv()
    copy = window_swap(3, core)
    copy.start()
    sends.append(copy)
    end_swap(0)
    vertical_step(0)
    window_arrival(2).wait_recv()
    copy = window_swap(2, core)
    copy.start()
    sends.append(copy)
    window_arrival(5).wait_recv()
    copy = window_swap(5, core)
    copy.start()
    sends.append(copy)
    arrive(1)
    arrive(3)
    window_swap(2, 1 - core).wait_recv()
    window_swap(3, 1 - core).wait_recv()
    slash_middle()
    end_swap(1)
    vertical_step(1)
    end_swap(3)
    vertical_step(3)
    arrive(2)
    window_swap(1, 1 - core).wait_recv()
    window_swap(5, 1 - core).wait_recv()
    slash_far()
    end_swap(2)
    vertical_step(2)

    for b in range(8):
        for h in range(2):
            rows = pl.ds(b * 128 + h * 64, 64)
            out[pl.ds(b * 64, 64), pl.ds(h * 128, 128)] = (acc[rows, :128] / acc[rows, 128:]).astype(BF16)

    for copy in sends:
        copy.wait_send()


def on_device(queries, stretch_kv, prefix_kv, vertical, slash_offsets, block_home):
    anywhere = pl.BlockSpec(memory_space=pl.ANY)
    dma = pltpu.SemaphoreType.DMA
    return pl.pallas_call(
        kernel,
        out_shape=jax.ShapeDtypeStruct((512, 256), BF16),
        in_specs=[anywhere] * 6,
        out_specs=pl.BlockSpec(memory_space=pltpu.VMEM),
        scratch_shapes=[
            pltpu.SMEM((8, 64), jnp.int32),
            pltpu.SMEM((32, 32), jnp.int32),
            pltpu.SMEM((1024,), jnp.int32),
            pltpu.VMEM((512, 16, 128), BF16),
            pltpu.VMEM((4096, 256), BF16),
            pltpu.VMEM((2048, 256), BF16),
            pltpu.VMEM((4, 512, 256), BF16),
            pltpu.VMEM((2, 3, 2, 128, 256), BF16),
            pltpu.VMEM((2, 2, 128, 256), BF16),
            pltpu.VMEM((2, 3, 2, 32, 256), BF16),
            pltpu.VMEM((128, 256), BF16),
            pltpu.VMEM((128, 256), BF16),
            pltpu.VMEM((4096, 256), BF16),
            pltpu.VMEM(((HOPS + 1) * 512, 256), BF16),
            pltpu.VMEM((8, 128, 128), BF16),
            pltpu.VMEM((8, BAND), F32),
            pltpu.VMEM((1024, 256), F32),
            pltpu.VMEM((1024, 128), F32),
            dma((6,)),
            dma((2, 3)), dma((2, 3)),
            dma((2, 3)), dma((2, 3)),
            dma((NZ - 1,)), dma((NZ - 1,)),
            dma((2, 3)), dma((2, 3)),
            dma((2, 3)), dma((2, 3)),
            dma((2, 4)), dma((2, 4)),
            dma((HOPS,)), dma((HOPS,)),
            dma((HOPS,)), dma((HOPS,)),
        ],
        compiler_params=pltpu.CompilerParams(
            collective_id=0, has_side_effects=True, vmem_limit_bytes=62 * 1024 * 1024
        ),
        cost_estimate=pl.CostEstimate(flops=7_000_000_000, bytes_accessed=6_000_000, transcendentals=7_000_000),
    )(
        queries,
        stretch_kv.reshape(-1, 256),
        prefix_kv.reshape(-1, 256),
        vertical,
        slash_offsets,
        block_home,
    )


def solution(mesh):
    return jax.shard_map(
        on_device,
        mesh=mesh,
        in_specs=(
            P("ctx", None, None),
            P("ctx", None, None),
            P(("ctx", "ksplit"), None, None, None),
            P(),
            P(),
            P(),
        ),
        out_specs=P("ctx", "ksplit"),
        check_vma=False,
    )
```

```python
import functools
import math

import jax
import jax.numpy as jnp
from jax import lax
from jax.experimental import pallas as pl
from jax.experimental.pallas import tpu as pltpu
from jax.sharding import PartitionSpec as P

MESH = pl.DeviceIdType.MESH
BLOCK = 64
NX = 4
NY = 4
NZ = 8
HOPS = 5
MASKED = -1e30
SCALE = math.log2(math.e) / math.sqrt(128.0)
BAND = 42 * BLOCK
F32 = jnp.float32
BF16 = jnp.bfloat16


def iota(shape, dim):
    return lax.broadcasted_iota(jnp.int32, shape, dim)


def kernel(
    q_hbm, s_hbm, p_hbm, vertical_hbm, offsets_hbm, home_hbm, out,
    vertical, offsets, home, xq, xs, xp, contrib, r1, p1, r2, fin, zr, vert, win, qb, band, acc, top,
    load_sem, r1_send, r1_recv, r2_send, r2_recv, z_send, z_recv,
    g1_send, g1_recv, g2_send, g2_recv, v_send, v_recv, w_send, w_recv, f_send, f_recv,
):
    c = lax.axis_index("ctx")
    s = lax.axis_index("ksplit")
    x, y = c // NY, c % NY
    z, core = s // 2, s % 2

    barrier = pltpu.get_barrier_semaphore()
    for k in range(1, 4):
        pl.semaphore_signal(barrier, inc=1, device_id=(((x + k) % NX) * NY + y, s), device_id_type=MESH)
        pl.semaphore_signal(barrier, inc=1, device_id=(x * NY + (y + k) % NY, s), device_id_type=MESH)
    for k in range(1, NZ):
        pl.semaphore_signal(barrier, inc=1, device_id=(c, ((z + k) % NZ) * 2 + core), device_id_type=MESH)
    pl.semaphore_signal(barrier, inc=1, device_id=(c, z * 2 + 1 - core), device_id_type=MESH)

    load_p = pltpu.make_async_copy(p_hbm, xp, load_sem.at[0])
    load_s = pltpu.make_async_copy(s_hbm, xs, load_sem.at[1])
    slab = pl.multiple_of((s // 8) * 16, 16)
    load_q = pltpu.make_async_copy(q_hbm.at[:, pl.ds(slab, 16), :], xq, load_sem.at[2])
    load_home = pltpu.make_async_copy(home_hbm, home, load_sem.at[3])
    load_vertical = pltpu.make_async_copy(vertical_hbm, vertical, load_sem.at[4])
    load_offsets = pltpu.make_async_copy(offsets_hbm, offsets, load_sem.at[5])
    load_home.start()
    load_vertical.start()
    load_offsets.start()
    load_p.start()
    load_s.start()
    load_q.start()

    load_home.wait()
    load_vertical.wait()
    load_offsets.wait()
    me = c * (2 * NZ) + s
    row16 = iota((16, 256), 0) % 8
    codes = []
    for v in range(4):
        code = jnp.full((16, 256), -1, jnp.int32)
        for g in range(8):
            slot = home[vertical[g, v * 2 * NZ + s]]
            here = jnp.where(slot // 4 == me, slot % 4, -1)
            code = jnp.where(row16 == g, here, code)
        codes.append(code)

    load_p.wait()
    for v in range(4):
        total = None
        for r in range(4):
            keep = jnp.where(codes[v] == r, 1.0, 0.0).astype(BF16)
            term = xp[pl.ds(r * 512, 512), :].reshape(32, 16, 256) * keep[None]
            total = term if total is None else total + term
        contrib[v] = total.reshape(512, 256)

    pl.semaphore_wait(barrier, 3 + 3 + NZ - 1 + 1)

    def along_x(k):
        return (((x + k) % NX) * NY + y, s)

    def along_y(k):
        return (x * NY + (y + k) % NY, s)

    sibling = (c, z * 2 + 1 - core)

    def remote(src, dst, send, recv, to):
        return pltpu.make_async_remote_copy(
            src_ref=src, dst_ref=dst, send_sem=send, recv_sem=recv, device_id=to, device_id_type=MESH
        )

    def first_round(half, k):
        to = along_x(k) if half == 0 else along_y(k)
        part = (x + k) % NX if half == 0 else (y + k) % NY
        src = contrib.at[pl.ds(2 * half, 2), pl.ds(pl.multiple_of(part * 128, 128), 128), :]
        return remote(src, r1.at[half, k - 1], r1_send.at[half, k - 1], r1_recv.at[half, k - 1], to)

    def second_round(half, k):
        to = along_y(k) if half == 0 else along_x(k)
        part = (y + k) % NY if half == 0 else (x + k) % NX
        src = p1.at[half, :, pl.ds(pl.multiple_of(part * 32, 32), 32), :]
        return remote(src, r2.at[half, k - 1], r2_send.at[half, k - 1], r2_recv.at[half, k - 1], to)

    order = (2, 1, 3)
    sends = []
    for k in order:
        for half in range(2):
            first_round(half, k).start()

    load_s.wait()
    pick_kv = jnp.where(iota((64, 512), 1) == iota((64, 512), 0) * 8 + z, 1.0, 0.0).astype(BF16)
    for b in range(8):
        picked = jnp.dot(pick_kv, xs[pl.ds(b * 512, 512), :], preferred_element_type=F32)
        win[pl.ds(HOPS * 512 + b * 64, 64), :] = picked.astype(BF16)

    def window_part(d, which):
        return win.at[pl.ds(pl.multiple_of((HOPS - d) * 512 + which * 256, 256), 256), :]

    def window_copy(d, held):
        to = along_x(1) if d >= 4 else along_y(d)
        return remote(window_part(held, core), window_part(d, core), w_send.at[d - 1], w_recv.at[d - 1], to)

    def window_arrival(d):
        return window_copy(d, d)

    def window_swap(d, which):
        part = window_part(d, which)
        return remote(part, part, f_send.at[d - 1], f_recv.at[d - 1], sibling)

    load_q.wait()
    i, j = iota((128, 1024), 0), iota((128, 1024), 1)
    pick_q = jnp.where(j == (i % 64) * 16 + 2 * (s % 8) + i // 64, 1.0, 0.0).astype(BF16)
    for b in range(8):
        slab_rows = xq[pl.ds(b * 64, 64)].reshape(1024, 128)
        qb[b] = jnp.dot(pick_q, slab_rows, preferred_element_type=F32).astype(BF16)

    rows = iota((8, BAND), 0)
    offset = 40 + (rows // 2) % 2 - iota((8, BAND), 1) // 64
    member = jnp.full((8, BAND), MASKED, F32)
    for n in range(32):
        first, second = offsets[2 * s, n], offsets[2 * s + 1, n]
        member = jnp.where(offset == jnp.where(rows % 2 == 0, first, second), 0.0, member)
    band[...] = member

    for half in range(2):
        for k in order:
            first_round(half, k).wait_send()
    copy = window_copy(4, 0)
    copy.start()
    sends.append(copy)
    for half in range(2):
        part = x if half == 0 else y
        total = contrib[pl.ds(2 * half, 2), pl.ds(pl.multiple_of(part * 128, 128), 128), :]
        for k in order:
            first_round(half, k).wait_recv()
            total = total + r1[half, k - 1]
        p1[half] = total
        for k in order:
            copy = second_round(half, k)
            copy.start()
            sends.append(copy)

    ends = []
    for half in range(2):
        part = y if half == 0 else x
        total = p1[half, :, pl.ds(pl.multiple_of(part * 32, 32), 32), :]
        for k in order:
            second_round(half, k).wait_recv()
            total = total + r2[half, k - 1]
        ends.append(total.reshape(64, 256))
    held = jnp.concatenate(ends, 0)
    i, j = iota((128, 128), 0), iota((128, 128), 1)
    by_head = jnp.where(i == (j % 8) * 16 + (j // 32) * 4 + (j % 32) // 8, 1.0, 0.0).astype(BF16)
    fin[...] = jnp.dot(by_head, held, preferred_element_type=F32).astype(BF16)

    def z_copy(k):
        there = (z + k) % NZ
        return remote(
            fin.at[pl.ds(pl.multiple_of(there * 16, 16), 16), :],
            zr.at[pl.ds(pl.multiple_of(z * 16, 16), 16), :],
            z_send.at[k - 1], z_recv.at[k - 1], (c, there * 2 + core),
        )

    def z_arrival(k):
        there = (z + NZ - k) % NZ
        place = zr.at[pl.ds(pl.multiple_of(there * 16, 16), 16), :]
        return remote(place, place, z_send.at[k - 1], z_recv.at[k - 1], (c, there * 2 + core))

    for k in (4, 3, 5, 2, 6, 1, 7):
        copy = z_copy(k)
        copy.start()
        sends.append(copy)
    def place(k, owner, half, start, count):
        return vert.at[pl.ds(pl.multiple_of(((k * 2 + owner) * 2 + half) * 256 + start, 64), count), :]

    def spread_one(half, k):
        to = along_y(k) if half == 0 else along_x(k)
        dst = place(0, core, half, k * 64, 64)
        return remote(place(0, core, half, 0, 64), dst, g1_send.at[half, k - 1], g1_recv.at[half, k - 1], to)

    def spread_two(half, k):
        to = along_x(k) if half == 0 else along_y(k)
        dst = place(k, core, half, 0, 256)
        return remote(place(0, core, half, 0, 256), dst, g2_send.at[half, k - 1], g2_recv.at[half, k - 1], to)

    def swap(half, k, owner):
        part = place(k, owner, half, 0, 256)
        return remote(part, part, v_send.at[half, k], v_recv.at[half, k], sibling)

    def start_swap(k):
        for half in range(2):
            copy = swap(half, k, core)
            copy.start()
            sends.append(copy)

    def end_swap(k):
        for half in range(2):
            swap(half, k, 1 - core).wait_recv()

    def arrive(k):
        for half in range(2):
            spread_two(half, k).wait_recv()
        start_swap(k)

    def attend(b, keys, bias=None, diagonal=False, first=False, last=False):
        rows = pl.ds(b * 128, 128)
        n = keys.shape[0]
        scores = lax.dot_general(qb[b], keys[:, :128], (((1,), (1,)), ((), ())), preferred_element_type=F32)
        if bias is not None:
            wide = [jnp.broadcast_to(bias[r : r + 1], (64, n)) for r in (2 * (b % 2), 2 * (b % 2) + 1)]
            scores = scores + jnp.concatenate(wide, 0)
        if diagonal:
            i, j = iota((128, 128), 0), iota((128, 128), 1)
            later = (j // 64 == b % 2) & (j % 64 > i % 64)
            tail = scores[:, n - 128 :] + jnp.where(later, MASKED, 0.0)
            scores = jnp.concatenate([scores[:, : n - 128], tail], 1)
        new = jnp.max(scores, 1, keepdims=True)
        if not first:
            old = top[rows, :]
            new = jnp.maximum(old, new)
        probs = jnp.exp2((scores - new[:, :1]) * SCALE).astype(BF16)
        values = jnp.concatenate([keys[:, 128:], jnp.ones((n, 128), BF16)], 1)
        add = jnp.dot(probs, values, preferred_element_type=F32)
        if first:
            top[rows, :] = jnp.broadcast_to(new, (128, 128))
            acc[rows, :] = add
        else:
            fade = jnp.exp2((old - new) * SCALE)
            total = acc[rows, :] * jnp.concatenate([fade, fade], 1) + add
            if last:
                result = (total[:, :128] / total[:, 128:]).astype(BF16)
                out[pl.ds(b * 64, 64), :] = jnp.concatenate([result[:64], result[64:]], 1)
            else:
                top[rows, :] = new
                acc[rows, :] = total

    def band_part(start, count, d):
        return band[:, pl.ds(start, count)] + jnp.where(c >= d, 0.0, MASKED)

    def slash_near():
        for b in range(8):
            p = b // 2
            keys = jnp.concatenate([win[pl.ds(512, 512), :], win[pl.ds(2560, 128 * p + 128), :]], 0)
            bias = [band_part(512 - 128 * p, 512, 4), band_part(2560 - 128 * p, 128 * p + 128, 0)]
            attend(b, keys, jnp.concatenate(bias, 1), diagonal=True, first=True)

    def slash_middle():
        for b in range(8):
            p = b // 2
            bias = [band_part(1024 - 128 * p, 512, 3), band_part(1536 - 128 * p, 512, 2)]
            attend(b, win[pl.ds(1024, 1024), :], jnp.concatenate(bias, 1))

    def slash_far():
        for b in range(8):
            p = b // 2
            keys = jnp.concatenate([win[pl.ds(128 * p, 512 - 128 * p), :], win[pl.ds(2048, 512), :]], 0)
            bias = [band_part(0, 512 - 128 * p, 5), band_part(2048 - 128 * p, 512, 1)]
            attend(b, keys, jnp.concatenate(bias, 1))

    def vertical_step(k, last=False):
        for b in range(8):
            attend(b, vert[pl.ds(k * 1024, 1024), :], last=last)

    window_arrival(4).wait_recv()
    copy = window_copy(1, jnp.where(y + 1 < NY, 0, 4))
    copy.start()
    sends.append(copy)
    copy = window_copy(3, jnp.where(y + 3 < NY, 0, 4))
    copy.start()
    sends.append(copy)
    copy = window_swap(4, core)
    copy.start()
    sends.append(copy)
    mine = pl.ds(pl.multiple_of(z * 16, 16), 16)
    zr[mine, :] = fin[mine, :]
    for k in range(1, NZ):
        z_arrival(k).wait_recv()

    for half in range(2):
        start = pl.multiple_of((core * 2 + half) * 256, 256)
        vert[pl.ds(start, 64), :] = zr[pl.ds(half * 64, 64), :]
        for k in order:
            copy = spread_one(half, k)
            copy.start()
            sends.append(copy)

    copy = window_copy(2, jnp.where(y + 2 < NY, 0, 4))
    copy.start()
    sends.append(copy)
    window_arrival(1).wait_recv()
    copy = window_copy(5, 1)
    copy.start()
    sends.append(copy)
    copy = window_swap(1, core)
    copy.start()
    sends.append(copy)
    window_swap(4, 1 - core).wait_recv()
    slash_near()
    for half in range(2):
        for k in order:
            spread_one(half, k).wait_recv()
        for k in (1, 3, 2):
            copy = spread_two(half, k)
            copy.start()
            sends.append(copy)
    start_swap(0)
    window_arrival(3).wait_recv()
    copy = window_swap(3, core)
    copy.start()
    sends.append(copy)
    end_swap(0)
    vertical_step(0)
    window_arrival(2).wait_recv()
    copy = window_swap(2, core)
    copy.start()
    sends.append(copy)
    window_arrival(5).wait_recv()
    copy = window_swap(5, core)
    copy.start()
    sends.append(copy)
    window_swap(2, 1 - core).wait_recv()
    window_swap(3, 1 - core).wait_recv()
    slash_middle()
    arrive(1)
    arrive(3)
    window_swap(1, 1 - core).wait_recv()
    window_swap(5, 1 - core).wait_recv()
    slash_far()
    end_swap(1)
    vertical_step(1)
    arrive(2)
    end_swap(3)
    vertical_step(3)
    end_swap(2)
    vertical_step(2, last=True)

    for copy in sends:
        copy.wait_send()


def on_device(queries, stretch_kv, prefix_kv, vertical, slash_offsets, block_home):
    anywhere = pl.BlockSpec(memory_space=pl.ANY)
    dma = pltpu.SemaphoreType.DMA
    return pl.pallas_call(
        kernel,
        out_shape=jax.ShapeDtypeStruct((512, 256), BF16),
        in_specs=[anywhere] * 6,
        out_specs=pl.BlockSpec(memory_space=pltpu.VMEM),
        scratch_shapes=[
            pltpu.SMEM((8, 64), jnp.int32),
            pltpu.SMEM((32, 32), jnp.int32),
            pltpu.SMEM((1024,), jnp.int32),
            pltpu.VMEM((512, 16, 128), BF16),
            pltpu.VMEM((4096, 256), BF16),
            pltpu.VMEM((2048, 256), BF16),
            pltpu.VMEM((4, 512, 256), BF16),
            pltpu.VMEM((2, 3, 2, 128, 256), BF16),
            pltpu.VMEM((2, 2, 128, 256), BF16),
            pltpu.VMEM((2, 3, 2, 32, 256), BF16),
            pltpu.VMEM((128, 256), BF16),
            pltpu.VMEM((128, 256), BF16),
            pltpu.VMEM((4096, 256), BF16),
            pltpu.VMEM(((HOPS + 1) * 512, 256), BF16),
            pltpu.VMEM((8, 128, 128), BF16),
            pltpu.VMEM((8, BAND), F32),
            pltpu.VMEM((1024, 256), F32),
            pltpu.VMEM((1024, 128), F32),
            dma((6,)),
            dma((2, 3)), dma((2, 3)),
            dma((2, 3)), dma((2, 3)),
            dma((NZ - 1,)), dma((NZ - 1,)),
            dma((2, 3)), dma((2, 3)),
            dma((2, 3)), dma((2, 3)),
            dma((2, 4)), dma((2, 4)),
            dma((HOPS,)), dma((HOPS,)),
            dma((HOPS,)), dma((HOPS,)),
        ],
        compiler_params=pltpu.CompilerParams(
            collective_id=0, has_side_effects=True, vmem_limit_bytes=62 * 1024 * 1024
        ),
        cost_estimate=pl.CostEstimate(flops=7_000_000_000, bytes_accessed=6_000_000, transcendentals=7_000_000),
    )(
        queries,
        stretch_kv.reshape(-1, 256),
        prefix_kv.reshape(-1, 256),
        vertical,
        slash_offsets,
        block_home,
    )


def solution(mesh):
    return jax.shard_map(
        on_device,
        mesh=mesh,
        in_specs=(
            P("ctx", None, None),
            P("ctx", None, None),
            P(("ctx", "ksplit"), None, None, None),
            P(),
            P(),
            P(),
        ),
        out_specs=P("ctx", "ksplit"),
        check_vma=False,
    )
```

```python
import functools
import math

import jax
import jax.numpy as jnp
from jax import lax
from jax.experimental import pallas as pl
from jax.experimental.pallas import tpu as pltpu
from jax.sharding import PartitionSpec as P

MESH = pl.DeviceIdType.MESH
BLOCK = 64
NX = 4
NY = 4
NZ = 8
HOPS = 5
MASKED = -1e30
SCALE = math.log2(math.e) / math.sqrt(128.0)
BAND = 42 * BLOCK
F32 = jnp.float32
BF16 = jnp.bfloat16


def iota(shape, dim):
    return lax.broadcasted_iota(jnp.int32, shape, dim)


def kernel(
    q_hbm, s_hbm, p_hbm, vertical_hbm, offsets_hbm, home_hbm, out,
    vertical, offsets, home, xq, xs, xp, contrib, r1, p1, r2, fin, zr, vert, win, qb, band, acc, top,
    load_sem, r1_send, r1_recv, r2_send, r2_recv, z_send, z_recv,
    g1_send, g1_recv, g2_send, g2_recv, v_send, v_recv, w_send, w_recv, f_send, f_recv,
):
    c = lax.axis_index("ctx")
    s = lax.axis_index("ksplit")
    x, y = c // NY, c % NY
    z, core = s // 2, s % 2

    barrier = pltpu.get_barrier_semaphore()
    for k in range(1, 4):
        pl.semaphore_signal(barrier, inc=1, device_id=(((x + k) % NX) * NY + y, s), device_id_type=MESH)
        pl.semaphore_signal(barrier, inc=1, device_id=(x * NY + (y + k) % NY, s), device_id_type=MESH)
    for k in range(1, NZ):
        pl.semaphore_signal(barrier, inc=1, device_id=(c, ((z + k) % NZ) * 2 + core), device_id_type=MESH)
    pl.semaphore_signal(barrier, inc=1, device_id=(c, z * 2 + 1 - core), device_id_type=MESH)

    load_p = pltpu.make_async_copy(p_hbm, xp, load_sem.at[0])
    load_s = pltpu.make_async_copy(s_hbm, xs, load_sem.at[1])
    slab = pl.multiple_of((s // 8) * 16, 16)
    load_q = pltpu.make_async_copy(q_hbm.at[:, pl.ds(slab, 16), :], xq, load_sem.at[2])
    load_home = pltpu.make_async_copy(home_hbm, home, load_sem.at[3])
    load_vertical = pltpu.make_async_copy(vertical_hbm, vertical, load_sem.at[4])
    load_offsets = pltpu.make_async_copy(offsets_hbm, offsets, load_sem.at[5])
    load_home.start()
    load_vertical.start()
    load_offsets.start()
    load_p.start()
    load_s.start()
    load_q.start()

    load_home.wait()
    load_vertical.wait()
    load_offsets.wait()
    me = c * (2 * NZ) + s
    row16 = iota((16, 256), 0) % 8
    codes = []
    for v in range(4):
        code = jnp.full((16, 256), -1, jnp.int32)
        for g in range(8):
            slot = home[vertical[g, v * 2 * NZ + s]]
            here = jnp.where(slot // 4 == me, slot % 4, -1)
            code = jnp.where(row16 == g, here, code)
        codes.append(code)

    load_p.wait()
    for v in range(4):
        total = None
        for r in range(4):
            keep = jnp.where(codes[v] == r, 1.0, 0.0).astype(BF16)
            term = xp[pl.ds(r * 512, 512), :].reshape(32, 16, 256) * keep[None]
            total = term if total is None else total + term
        contrib[v] = total.reshape(512, 256)

    pl.semaphore_wait(barrier, 3 + 3 + NZ - 1 + 1)

    def along_x(k):
        return (((x + k) % NX) * NY + y, s)

    def along_y(k):
        return (x * NY + (y + k) % NY, s)

    sibling = (c, z * 2 + 1 - core)

    def remote(src, dst, send, recv, to):
        return pltpu.make_async_remote_copy(
            src_ref=src, dst_ref=dst, send_sem=send, recv_sem=recv, device_id=to, device_id_type=MESH
        )

    def first_round(half, k):
        to = along_x(k) if half == 0 else along_y(k)
        part = (x + k) % NX if half == 0 else (y + k) % NY
        src = contrib.at[pl.ds(2 * half, 2), pl.ds(pl.multiple_of(part * 128, 128), 128), :]
        return remote(src, r1.at[half, k - 1], r1_send.at[half, k - 1], r1_recv.at[half, k - 1], to)

    def second_round(half, k):
        to = along_y(k) if half == 0 else along_x(k)
        part = (y + k) % NY if half == 0 else (x + k) % NX
        src = p1.at[half, :, pl.ds(pl.multiple_of(part * 32, 32), 32), :]
        return remote(src, r2.at[half, k - 1], r2_send.at[half, k - 1], r2_recv.at[half, k - 1], to)

    order = (2, 1, 3)
    sends = []
    for k in order:
        for half in range(2):
            first_round(half, k).start()

    load_s.wait()
    pick_kv = jnp.where(iota((64, 512), 1) == iota((64, 512), 0) * 8 + z, 1.0, 0.0).astype(BF16)
    for b in range(8):
        picked = jnp.dot(pick_kv, xs[pl.ds(b * 512, 512), :], preferred_element_type=F32)
        win[pl.ds(HOPS * 512 + b * 64, 64), :] = picked.astype(BF16)

    def window_part(d, which):
        return win.at[pl.ds(pl.multiple_of((HOPS - d) * 512 + which * 256, 256), 256), :]

    def window_copy(d, held):
        to = along_x(1) if d >= 4 else along_y(d)
        return remote(window_part(held, core), window_part(d, core), w_send.at[d - 1], w_recv.at[d - 1], to)

    def window_arrival(d):
        return window_copy(d, d)

    def window_swap(d, which):
        part = window_part(d, which)
        return remote(part, part, f_send.at[d - 1], f_recv.at[d - 1], sibling)

    load_q.wait()
    i, j = iota((128, 1024), 0), iota((128, 1024), 1)
    pick_q = jnp.where(j == (i % 64) * 16 + 2 * (s % 8) + i // 64, 1.0, 0.0).astype(BF16)
    for b in range(8):
        slab_rows = xq[pl.ds(b * 64, 64)].reshape(1024, 128)
        qb[b] = jnp.dot(pick_q, slab_rows, preferred_element_type=F32).astype(BF16)

    rows = iota((8, BAND), 0)
    offset = 40 + (rows // 2) % 2 - iota((8, BAND), 1) // 64
    member = jnp.full((8, BAND), MASKED, F32)
    for n in range(32):
        first, second = offsets[2 * s, n], offsets[2 * s + 1, n]
        member = jnp.where(offset == jnp.where(rows % 2 == 0, first, second), 0.0, member)
    band[...] = member

    for half in range(2):
        for k in order:
            first_round(half, k).wait_send()
    copy = window_copy(4, 0)
    copy.start()
    sends.append(copy)
    for half in range(2):
        part = x if half == 0 else y
        total = contrib[pl.ds(2 * half, 2), pl.ds(pl.multiple_of(part * 128, 128), 128), :]
        for k in order:
            first_round(half, k).wait_recv()
            total = total + r1[half, k - 1]
        p1[half] = total
        for k in order:
            copy = second_round(half, k)
            copy.start()
            sends.append(copy)

    ends = []
    for half in range(2):
        part = y if half == 0 else x
        total = p1[half, :, pl.ds(pl.multiple_of(part * 32, 32), 32), :]
        for k in order:
            second_round(half, k).wait_recv()
            total = total + r2[half, k - 1]
        ends.append(total.reshape(64, 256))
    held = jnp.concatenate(ends, 0)
    i, j = iota((128, 128), 0), iota((128, 128), 1)
    by_head = jnp.where(i == (j % 8) * 16 + (j // 32) * 4 + (j % 32) // 8, 1.0, 0.0).astype(BF16)
    fin[...] = jnp.dot(by_head, held, preferred_element_type=F32).astype(BF16)

    def z_copy(k):
        there = (z + k) % NZ
        return remote(
            fin.at[pl.ds(pl.multiple_of(there * 16, 16), 16), :],
            zr.at[pl.ds(pl.multiple_of(z * 16, 16), 16), :],
            z_send.at[k - 1], z_recv.at[k - 1], (c, there * 2 + core),
        )

    def z_arrival(k):
        there = (z + NZ - k) % NZ
        place = zr.at[pl.ds(pl.multiple_of(there * 16, 16), 16), :]
        return remote(place, place, z_send.at[k - 1], z_recv.at[k - 1], (c, there * 2 + core))

    for k in (4, 3, 5, 2, 6, 1, 7):
        copy = z_copy(k)
        copy.start()
        sends.append(copy)
    def place(k, owner, half, start, count):
        return vert.at[pl.ds(pl.multiple_of(((k * 2 + owner) * 2 + half) * 256 + start, 64), count), :]

    def spread_one(half, k):
        to = along_y(k) if half == 0 else along_x(k)
        dst = place(0, core, half, k * 64, 64)
        return remote(place(0, core, half, 0, 64), dst, g1_send.at[half, k - 1], g1_recv.at[half, k - 1], to)

    def spread_two(half, k):
        to = along_x(k) if half == 0 else along_y(k)
        dst = place(k, core, half, 0, 256)
        return remote(place(0, core, half, 0, 256), dst, g2_send.at[half, k - 1], g2_recv.at[half, k - 1], to)

    def swap(half, k, owner):
        part = place(k, owner, half, 0, 256)
        return remote(part, part, v_send.at[half, k], v_recv.at[half, k], sibling)

    def start_swap(k):
        for half in range(2):
            copy = swap(half, k, core)
            copy.start()
            sends.append(copy)

    def end_swap(k):
        for half in range(2):
            swap(half, k, 1 - core).wait_recv()

    def arrive(k):
        for half in range(2):
            spread_two(half, k).wait_recv()
        start_swap(k)

    def attend(b, keys, bias=None, diagonal=False, first=False, last=False):
        rows = pl.ds(b * 128, 128)
        n = keys.shape[0]
        scores = lax.dot_general(qb[b], keys[:, :128], (((1,), (1,)), ((), ())), preferred_element_type=F32)
        if bias is not None:
            wide = [jnp.broadcast_to(bias[r : r + 1], (64, n)) for r in (2 * (b % 2), 2 * (b % 2) + 1)]
            scores = scores + jnp.concatenate(wide, 0)
        if diagonal:
            i, j = iota((128, 128), 0), iota((128, 128), 1)
            later = (j // 64 == b % 2) & (j % 64 > i % 64)
            tail = scores[:, n - 128 :] + jnp.where(later, MASKED, 0.0)
            scores = jnp.concatenate([scores[:, : n - 128], tail], 1)
        new = jnp.max(scores, 1, keepdims=True)
        if not first:
            old = top[rows, :]
            new = jnp.maximum(old, new)
        probs = jnp.exp2((scores - new[:, :1]) * SCALE).astype(BF16)
        values = jnp.concatenate([keys[:, 128:], jnp.ones((n, 128), BF16)], 1)
        add = jnp.dot(probs, values, preferred_element_type=F32)
        if first:
            top[rows, :] = jnp.broadcast_to(new, (128, 128))
            acc[rows, :] = add
        else:
            fade = jnp.exp2((old - new) * SCALE)
            total = acc[rows, :] * jnp.concatenate([fade, fade], 1) + add
            if last:
                result = (total[:, :128] / total[:, 128:]).astype(BF16)
                out[pl.ds(b * 64, 64), :] = jnp.concatenate([result[:64], result[64:]], 1)
            else:
                top[rows, :] = new
                acc[rows, :] = total

    def band_part(start, count, d):
        return band[:, pl.ds(start, count)] + jnp.where(c >= d, 0.0, MASKED)

    def slash_near():
        for b in range(8):
            p = b // 2
            keys = jnp.concatenate([win[pl.ds(512, 512), :], win[pl.ds(2560, 128 * p + 128), :]], 0)
            bias = [band_part(512 - 128 * p, 512, 4), band_part(2560 - 128 * p, 128 * p + 128, 0)]
            attend(b, keys, jnp.concatenate(bias, 1), diagonal=True, first=True)

    def slash_middle():
        for b in range(8):
            p = b // 2
            bias = [band_part(1024 - 128 * p, 512, 3), band_part(1536 - 128 * p, 512, 2)]
            attend(b, win[pl.ds(1024, 1024), :], jnp.concatenate(bias, 1))

    def slash_far():
        for b in range(8):
            p = b // 2
            keys = jnp.concatenate([win[pl.ds(128 * p, 512 - 128 * p), :], win[pl.ds(2048, 512), :]], 0)
            bias = [band_part(0, 512 - 128 * p, 5), band_part(2048 - 128 * p, 512, 1)]
            attend(b, keys, jnp.concatenate(bias, 1))

    def vertical_step(k, last=False):
        for b in range(8):
            attend(b, vert[pl.ds(k * 1024, 1024), :], last=last)

    window_arrival(4).wait_recv()
    copy = window_copy(1, jnp.where(y + 1 < NY, 0, 4))
    copy.start()
    sends.append(copy)
    copy = window_copy(3, jnp.where(y + 3 < NY, 0, 4))
    copy.start()
    sends.append(copy)
    copy = window_swap(4, core)
    copy.start()
    sends.append(copy)
    mine = pl.ds(pl.multiple_of(z * 16, 16), 16)
    zr[mine, :] = fin[mine, :]
    for k in range(1, NZ):
        z_arrival(k).wait_recv()

    for half in range(2):
        start = pl.multiple_of((core * 2 + half) * 256, 256)
        vert[pl.ds(start, 64), :] = zr[pl.ds(half * 64, 64), :]
        for k in order:
            copy = spread_one(half, k)
            copy.start()
            sends.append(copy)

    copy = window_copy(2, jnp.where(y + 2 < NY, 0, 4))
    copy.start()
    sends.append(copy)
    window_arrival(1).wait_recv()
    copy = window_copy(5, 1)
    copy.start()
    sends.append(copy)
    copy = window_swap(1, core)
    copy.start()
    sends.append(copy)
    window_swap(4, 1 - core).wait_recv()
    slash_near()
    for half in range(2):
        for k in order:
            spread_one(half, k).wait_recv()
        for k in (1, 3, 2):
            copy = spread_two(half, k)
            copy.start()
            sends.append(copy)
    start_swap(0)
    window_arrival(3).wait_recv()
    copy = window_swap(3, core)
    copy.start()
    sends.append(copy)
    end_swap(0)
    vertical_step(0)
    window_arrival(2).wait_recv()
    copy = window_swap(2, core)
    copy.start()
    sends.append(copy)
    window_swap(2, 1 - core).wait_recv()
    window_swap(3, 1 - core).wait_recv()
    slash_middle()
    window_arrival(5).wait_recv()
    copy = window_swap(5, core)
    copy.start()
    sends.append(copy)
    arrive(1)
    arrive(3)
    window_swap(1, 1 - core).wait_recv()
    window_swap(5, 1 - core).wait_recv()
    slash_far()
    end_swap(1)
    vertical_step(1)
    arrive(2)
    end_swap(3)
    vertical_step(3)
    end_swap(2)
    vertical_step(2, last=True)

    for copy in sends:
        copy.wait_send()


def on_device(queries, stretch_kv, prefix_kv, vertical, slash_offsets, block_home):
    anywhere = pl.BlockSpec(memory_space=pl.ANY)
    dma = pltpu.SemaphoreType.DMA
    return pl.pallas_call(
        kernel,
        out_shape=jax.ShapeDtypeStruct((512, 256), BF16),
        in_specs=[anywhere] * 6,
        out_specs=pl.BlockSpec(memory_space=pltpu.VMEM),
        scratch_shapes=[
            pltpu.SMEM((8, 64), jnp.int32),
            pltpu.SMEM((32, 32), jnp.int32),
            pltpu.SMEM((1024,), jnp.int32),
            pltpu.VMEM((512, 16, 128), BF16),
            pltpu.VMEM((4096, 256), BF16),
            pltpu.VMEM((2048, 256), BF16),
            pltpu.VMEM((4, 512, 256), BF16),
            pltpu.VMEM((2, 3, 2, 128, 256), BF16),
            pltpu.VMEM((2, 2, 128, 256), BF16),
            pltpu.VMEM((2, 3, 2, 32, 256), BF16),
            pltpu.VMEM((128, 256), BF16),
            pltpu.VMEM((128, 256), BF16),
            pltpu.VMEM((4096, 256), BF16),
            pltpu.VMEM(((HOPS + 1) * 512, 256), BF16),
            pltpu.VMEM((8, 128, 128), BF16),
            pltpu.VMEM((8, BAND), F32),
            pltpu.VMEM((1024, 256), F32),
            pltpu.VMEM((1024, 128), F32),
            dma((6,)),
            dma((2, 3)), dma((2, 3)),
            dma((2, 3)), dma((2, 3)),
            dma((NZ - 1,)), dma((NZ - 1,)),
            dma((2, 3)), dma((2, 3)),
            dma((2, 3)), dma((2, 3)),
            dma((2, 4)), dma((2, 4)),
            dma((HOPS,)), dma((HOPS,)),
            dma((HOPS,)), dma((HOPS,)),
        ],
        compiler_params=pltpu.CompilerParams(
            collective_id=0, has_side_effects=True, vmem_limit_bytes=62 * 1024 * 1024
        ),
        cost_estimate=pl.CostEstimate(flops=7_000_000_000, bytes_accessed=6_000_000, transcendentals=7_000_000),
    )(
        queries,
        stretch_kv.reshape(-1, 256),
        prefix_kv.reshape(-1, 256),
        vertical,
        slash_offsets,
        block_home,
    )


def solution(mesh):
    return jax.shard_map(
        on_device,
        mesh=mesh,
        in_specs=(
            P("ctx", None, None),
            P("ctx", None, None),
            P(("ctx", "ksplit"), None, None, None),
            P(),
            P(),
            P(),
        ),
        out_specs=P("ctx", "ksplit"),
        check_vma=False,
    )
```
